128 devices in a mesh: attn: 32 (over y, z, core), exp: 4 (over x).
Axes of the slice: x: 4, y: 4, z: 4, core: 2. Of those that a mesh axis runs over, the one named last changes fastest.
Arguments:
- hidden: bfloat16 [1024, 7168], P(('attn', 'exp')), may hold values from -6 to 6
- norm_gain: float32 [7168], replicated, may hold values from 0.1 to 1.9
- routes: int32 [1024, 8], P(('attn', 'exp')), may hold values from 0 to 31, all different within a row; in each aligned block of 4 rows (0 to 3, 4 to 7, ...) at most 2 rows name the same one
- route_scores: float32 [1024, 8], P(('attn', 'exp')), may hold values from 0.1 to 1
- capacity: int32 [32], replicated, may hold values from 1 to 2
- w_gate: bfloat16 [32, 7168, 2048], P('attn', 'exp'), may hold values from -0.0625 to 0.0625
- w_up: bfloat16 [32, 7168, 2048], P('attn', 'exp'), may hold values from -0.0625 to 0.0625
- w_down: bfloat16 [32, 2048, 7168], P('attn', None, 'exp'), may hold values from -0.125 to 0.125
Outputs:
- moe_out: bfloat16 [1024, 7168], P(('attn', 'exp'))
The draws below stay inside these ranges and needn't reach their ends.
Inputs may be any that keep to these rules, and one draw needn't show every extreme that they name: `routes`: each row names 8 different experts; in each aligned block of 4 rows no expert is named by more than 2 rows, and in some block some expert is named by exactly 2 rows.
All inputs are finite; a program needn't handle non-finite values.
Results may differ from the reference program's by a relative error of at most 0.015.
Values may be sent and summed in bfloat16 or wider, within the bound.
No kernel may reach another device: no remote copies, remote signals or barrier semaphores. Data moves between devices by JAX's collectives and lax.ppermute only.
A program may use at most 128 MiB of HBM per device.

```python
import math
import jax
import jax.numpy as jnp
import numpy as np
from jax import lax

D = 7168
FF = 2048
TOP = 8
MICRO = 2
RM = 4
EXPERTS = 32
CAP = 2
ROWS = 1024
N_EXP = 4
DEVICES = 128


def touch_ends(drawn, key, low, largest):
    extent = drawn.shape
    place = [jax.random.randint(jax.random.fold_in(key, axis), (), 0, extent[axis]) for axis in range(len(extent))]
    drawn = drawn.at[tuple(place)].set(low)
    longest = extent.index(max(extent))
    place[longest] = (place[longest] + 1) % extent[longest]
    return drawn.at[tuple(place)].set(largest)


def level_of(stream_key, shape, shards, low, top_value):
    factor_of = 1.0
    for axis_at, shards_of in shards:
        heights = jax.random.uniform(jax.random.fold_in(jax.random.fold_in(stream_key, 6), axis_at), (shards_of,), jnp.float32, low / len(shards), top_value / len(shards))
        factor_of = factor_of * jnp.repeat(jnp.exp(heights), shape[axis_at] // shards_of).reshape((-1,) + (1,) * (len(shape) - 1 - axis_at))
    return factor_of


def routed_block(key, own, number, rows, number_of, top, most, lean):
    order = jax.random.permutation(key, number_of)
    crowded, ordinary = portions_of(number_of, rows * top, most, lean, True), portions_of(number_of, rows * top, most, lean, False)
    places = jnp.arange(number_of)

    def named(lengths, turn):
        used = int((lengths > 0).sum())
        fixed = max(1, used // 4)
        passed = fixed + (places - fixed + turn * (used - fixed)) % max(1, number_of - fixed)
        return jnp.zeros((number_of,), jnp.int32).at[order[jnp.where(places < fixed, places, passed)]].set(jnp.asarray(lengths, jnp.int32))

    lengths = jnp.where(number % 4 == 0, named(crowded, number // 4), named(ordinary, number - number // 4 - 1))
    mixed = jax.random.permutation(jax.random.fold_in(own, 3), number_of)
    source_of, sink = mixed[0:number_of // 2 * 2:2], mixed[1:number_of // 2 * 2:2]
    room = jnp.minimum(lengths[source_of] - 1, most - lengths[sink]) // 2
    room = jnp.where((source_of == order[0]) | (sink == order[0]) | (lengths[sink] == 0), 0, jnp.maximum(room, 0))
    passed = jax.random.randint(jax.random.fold_in(own, 4), (number_of // 2,), 0, 1 << 20) % (room + 1)
    lengths = lengths.at[source_of].add(-passed).at[sink].add(passed)
    members = jnp.searchsorted(jnp.cumsum(lengths), jnp.arange(rows * top), side="right").astype(jnp.int32)
    table = members.reshape(top, rows).T
    table = table[jax.random.permutation(jax.random.fold_in(own, 1), rows)]
    turn = jax.random.randint(jax.random.fold_in(own, 2), (rows, 1), 0, top)
    return jnp.take_along_axis(table, (jnp.arange(top)[None, :] + turn) % top, axis=1)


def portions_of(count, total, most, slope, full):
    portions = [(1 << 20) // math.isqrt(grade ** slope) + 1 for grade in range(1, count + 1)]
    largest = most if full else min(most, max(-(-total // count), total * portions[0] // sum(portions)))
    least = 1 if total - largest >= count - 1 else 0
    given, rest = [largest] + [least] * (count - 1), total - largest - least * (count - 1)
    while rest > 0:
        movable = [i for i in range(1, count) if given[i] < largest] or [i for i in range(1, count) if given[i] < most]
        mass, budget = sum([portions[i] for i in movable]), rest
        for i in movable:
            extra = min(most - given[i], max(1, budget * portions[i] // mass), rest)
            given[i] = given[i] + extra
            rest = rest - extra
    return np.array(given)


def bell_draw(own_key, dims, spread, bound, shards=(), held_as=jnp.bfloat16):
    array = jax.random.normal(own_key, dims, jnp.float32) * spread
    if len(shards) > 0:
        array = level_of(own_key, dims, shards, -0.22, 0.18) * array
    return jnp.clip(array, min=-bound, max=bound).astype(held_as)


def setup_inputs(seed: int = 0) -> dict:
    arg_keys = jax.random.split(jax.random.key(seed), 9)
    hidden = bell_draw(arg_keys[0], (ROWS, D), 1.0, 6.0, ((0, 128),))
    norm_gain = jnp.clip(1.0 + 0.18 * jax.random.normal(arg_keys[1], (D,), jnp.float32), 0.1, 1.9)
    routes_keys = jax.random.split(jax.random.fold_in(arg_keys[2], 1), ROWS // RM)
    routes_turns = jax.random.permutation(jax.random.fold_in(arg_keys[2], 3), ROWS // RM)
    routes = jax.vmap(lambda own, number: routed_block(jax.random.fold_in(arg_keys[2], 2), own, number, RM, EXPERTS, TOP, CAP, 2))(routes_keys, routes_turns).reshape((ROWS, TOP))
    route_scores = jnp.clip(0.1 + 0.9 * jax.random.uniform(arg_keys[3], (ROWS, TOP), jnp.float32) ** level_of(arg_keys[3], (ROWS, TOP), ((0, 128),), -0.2, 0.2), 0.1, 1.0)
    capacity = touch_ends(jax.random.randint(arg_keys[4], (EXPERTS,), 1, CAP + 1), jax.random.fold_in(arg_keys[4], 1), 1, CAP).astype(jnp.int32)
    w_gate = bell_draw(arg_keys[5], (EXPERTS, D, FF), D ** -0.5, 0.0625, ((0, 32), (1, 4)))
    w_up = bell_draw(arg_keys[6], (EXPERTS, D, FF), D ** -0.5, 0.0625, ((0, 32), (1, 4)))
    w_down = bell_draw(arg_keys[7], (EXPERTS, FF, D), FF ** -0.5, 0.125, ((0, 32), (2, 4)))
    return {"hidden": hidden, "norm_gain": norm_gain, "routes": routes, "route_scores": route_scores, "capacity": capacity, "w_gate": w_gate, "w_up": w_up, "w_down": w_down}


ROUTE_SCALE = 2.5
EPSILON = 1e-06

def round_partial(value):
    return lax.optimization_barrier(value.astype(jnp.bfloat16)).astype(jnp.float32)

def expert_rows(packed):
    rows_in, gate_w, up_w, down_w = packed
    slot_total = rows_in.shape[0]
    split_rows = rows_in.reshape(slot_total, N_EXP, D // N_EXP).astype(jnp.float32)
    gate_parts = jnp.einsum('mad,adf->amf', split_rows, gate_w.reshape(N_EXP, D // N_EXP, FF).astype(jnp.float32))
    up_parts = jnp.einsum('mad,adf->amf', split_rows, up_w.reshape(N_EXP, D // N_EXP, FF).astype(jnp.float32))
    gate_sum = lax.optimization_barrier(jnp.sum(round_partial(gate_parts), axis=0))
    up_sum = lax.optimization_barrier(jnp.sum(round_partial(up_parts), axis=0))
    activation = (jax.nn.silu(gate_sum) * up_sum).astype(jnp.bfloat16)
    return jnp.dot(activation, down_w, preferred_element_type=jnp.float32).astype(jnp.bfloat16)

def reference(hidden, norm_gain, routes, route_scores, capacity, w_gate, w_up, w_down):
    block_total = DEVICES * MICRO
    hidden_f = hidden.astype(jnp.float32)
    normed = (hidden_f * lax.rsqrt(lax.optimization_barrier(jnp.mean(hidden_f * hidden_f, axis=1, keepdims=True)) + EPSILON) * norm_gain).astype(jnp.bfloat16)
    route_weights = ROUTE_SCALE * route_scores / lax.optimization_barrier(jnp.sum(route_scores, axis=1, keepdims=True))
    block_ids = routes.reshape(block_total, RM * TOP).astype(jnp.int32)
    onehot = (block_ids[:, :, None] == jnp.arange(EXPERTS, dtype=jnp.int32)[None, None, :]).astype(jnp.int32)
    earlier = jnp.cumsum(onehot, axis=1) - onehot
    pair_rank = lax.optimization_barrier(jnp.sum(earlier * onehot, axis=2)).astype(jnp.int32)
    kept_mask = pair_rank < capacity[block_ids]
    slot_ids = jnp.where(kept_mask, block_ids * CAP + pair_rank, EXPERTS * CAP).astype(jnp.int32)
    source_rows = jnp.repeat(normed.reshape(block_total, RM, D), TOP, axis=1)
    block_index = jnp.broadcast_to(jnp.arange(block_total, dtype=jnp.int32)[:, None], slot_ids.shape)
    buffers = jnp.zeros((block_total, EXPERTS * CAP, D), jnp.bfloat16).at[block_index, slot_ids].set(source_rows, mode='drop')
    per_expert = buffers.reshape(block_total, EXPERTS, CAP, D).transpose(1, 0, 2, 3).reshape(EXPERTS, block_total * CAP, D)
    results = lax.map(expert_rows, (per_expert, w_gate, w_up, w_down))
    returned = results.reshape(EXPERTS, block_total, CAP, D).transpose(1, 0, 2, 3).reshape(block_total, EXPERTS * CAP, D)
    picked = returned[block_index, jnp.minimum(slot_ids, EXPERTS * CAP - 1)].astype(jnp.float32)
    pair_weights = jnp.where(kept_mask, route_weights.reshape(block_total, RM * TOP), 0.0)
    moe_sum = lax.optimization_barrier(jnp.sum((pair_weights[:, :, None] * picked).reshape(block_total, RM, TOP, D), axis=2))
    moe_out = (hidden_f + moe_sum.reshape(ROWS, D)).astype(jnp.bfloat16)
    return moe_out
```

```python
import jax
import jax.numpy as jnp
from jax import lax
from jax.sharding import Mesh, PartitionSpec as P

MICRO = 2
ROUTE_SCALE = 2.5
EPSILON = 1e-06
PAD = 128
RING = 4


def move(value, step):
    return lax.ppermute(value, "x", [(i, (i + step) % RING) for i in range(RING)])


def swap(value, axes):
    return lax.all_to_all(value, axes, split_axis=0, concat_axis=0, tiled=True)


def add(one, other):
    return (one.astype(jnp.float32) + other.astype(jnp.float32)).astype(jnp.bfloat16)


def routing_columns(routes, route_scores, capacity):
    rows, experts = routes.shape[0], capacity.shape[0]
    weights = ROUTE_SCALE * route_scores / jnp.sum(route_scores, axis=1, keepdims=True)
    named = routes[:, :, None] == jnp.arange(experts, dtype=jnp.int32)[None, None, :]
    match = jnp.any(named, axis=1)
    weight = jnp.sum(jnp.where(named, weights[:, :, None], 0.0), axis=1)
    blocks = match.astype(jnp.int32).reshape(rows // 4, 4, experts)
    running = jnp.zeros((rows // 4, experts), jnp.int32)
    ranks = []
    for row in range(4):
        ranks.append(running)
        running = running + blocks[:, row]
    rank = jnp.stack(ranks, axis=1).reshape(rows, experts)
    kept = match & (rank < capacity[None, :])
    code = jnp.where(kept, rank + 1, 0).astype(jnp.bfloat16)
    weight = jnp.where(kept, weight, 0.0)
    high = lax.reduce_precision(weight, 8, 7)
    low = weight - high
    empty = jnp.zeros((rows, PAD - 3 * experts), jnp.bfloat16)
    return jnp.concatenate([code, high.astype(jnp.bfloat16), low.astype(jnp.bfloat16), empty], axis=1)


def slot_maps(picks, targets, experts):
    rows = picks.shape[0]
    slot = jnp.arange(8 * rows // 2, dtype=jnp.int32)
    target = targets(slot // (rows // 2))
    lane = jnp.arange(PAD, dtype=jnp.int32)[:, None]
    parts = [
        jnp.dot(picks, (lane == target[None, :] + k * experts).astype(jnp.bfloat16), preferred_element_type=jnp.float32)
        for k in range(3)
    ]
    row = jnp.arange(rows, dtype=jnp.int32)
    chosen = (row[:, None] // 4 == slot[None, :] % (rows // 2) // 2) & (
        parts[0].astype(jnp.int32) == (slot % 2 + 1)[None, :]
    )
    return (
        chosen.astype(jnp.bfloat16),
        jnp.where(chosen, parts[1], 0.0).astype(jnp.bfloat16),
        jnp.where(chosen, parts[2], 0.0).astype(jnp.bfloat16),
    )


def shards(hidden, norm_gain, routes, route_scores, capacity, w_gate, w_up, w_down):
    experts = capacity.shape[0]
    place = lax.axis_index("x")
    width = w_gate.shape[1]
    ff = w_gate.shape[2]
    rows = hidden.shape[0]
    micro_rows = rows // MICRO
    hidden_f = hidden.astype(jnp.float32)
    normed = (
        hidden_f
        * lax.rsqrt(jnp.mean(hidden_f * hidden_f, axis=1, keepdims=True) + EPSILON)
        * norm_gain
    ).astype(jnp.bfloat16)
    columns = routing_columns(routes, route_scores, capacity)
    payload = jnp.stack(
        [jnp.concatenate([normed[:, r * width : (r + 1) * width], columns], axis=1) for r in range(RING)]
    )
    mixed = swap(payload, "x")
    entering, maps = [], []
    for micro in range(MICRO):
        first, second = ("y", "z") if micro == 0 else ("z", "y")
        lines = mixed[:, micro * micro_rows : (micro + 1) * micro_rows].reshape(1, RING * micro_rows, width + PAD)
        lines = swap(jnp.broadcast_to(lines, (RING,) + lines.shape[1:]), first)
        lines = lines.reshape(RING * RING * micro_rows, width + PAD)
        if micro == 0:
            targets = lambda far: lax.axis_index("y") * 8 + far
        else:
            targets = lambda far: far // 2 * 8 + lax.axis_index("z") * 2 + far % 2
        chosen, high, low = slot_maps(lines[:, width:], targets, experts)
        picked = lax.dot_general(
            chosen, lines[:, :width], (((0,), (0,)), ((), ())), preferred_element_type=jnp.float32
        ).astype(jnp.bfloat16)
        entering.append(swap(picked.reshape(8, -1, width), (second, "core")))
        maps.append((high, low))
    sums = []
    for micro in range(MICRO):
        first, second = ("y", "z") if micro == 0 else ("z", "y")
        slots = entering[micro].reshape(-1, width)
        gate = jnp.dot(slots, w_gate[0], preferred_element_type=jnp.float32).astype(jnp.bfloat16)
        up = jnp.dot(slots, w_up[0], preferred_element_type=jnp.float32).astype(jnp.bfloat16)
        part = slots.shape[0] // RING
        own = [lax.rem(place + r, RING) * part for r in range(RING)]
        gate = [lax.dynamic_slice_in_dim(gate, start, part, axis=0) for start in own]
        up = [lax.dynamic_slice_in_dim(up, start, part, axis=0) for start in own]
        gate_far = move(gate[2], 1)
        up_far = move(up[2], -1)
        up_low = move(up[1], 1)
        gate_high = move(gate[3], -1)
        gate_low = move(add(gate[1], gate_far), 1)
        up_high = move(add(up[3], up_far), -1)
        gate_sum = gate[0].astype(jnp.float32) + gate_low.astype(jnp.float32) + gate_high.astype(jnp.float32)
        up_sum = up[0].astype(jnp.float32) + up_low.astype(jnp.float32) + up_high.astype(jnp.float32)
        activation = (jax.nn.silu(gate_sum) * up_sum).astype(jnp.bfloat16)
        half = part // 2
        low = move(activation, 1)
        high = move(activation, -1)
        far_low = move(low[:half], 1)
        far_high = move(high[half:], -1)
        whole = jnp.zeros((RING * part, ff), jnp.bfloat16)
        for value, start in (
            (activation, own[0]), (high, own[1]), (far_low, own[2]), (far_high, own[2] + half), (low, own[3])
        ):
            whole = lax.dynamic_update_slice_in_dim(whole, value, start, axis=0)
        expert_out = jnp.dot(whole, w_down[0], preferred_element_type=jnp.float32).astype(jnp.bfloat16)
        returned = swap(expert_out.reshape(8, -1, width), (second, "core")).reshape(-1, width)
        high, low = maps[micro]
        spread = jnp.dot(high, returned, preferred_element_type=jnp.float32)
        spread += jnp.dot(low, returned, preferred_element_type=jnp.float32)
        spread = swap(spread.astype(jnp.bfloat16).reshape(RING, -1, width), first)
        summed = jnp.sum(spread.astype(jnp.float32), axis=0).astype(jnp.bfloat16)
        sums.append(summed.reshape(RING, micro_rows, width))
    back = swap(jnp.concatenate(sums, axis=1), "x")
    moe_sum = jnp.concatenate([back[r] for r in range(RING)], axis=1).astype(jnp.float32)
    return (hidden_f + moe_sum).astype(jnp.bfloat16)


def solution(mesh):
    fine = Mesh(mesh.devices.reshape(RING, RING, 2, RING), ("y", "z", "core", "x"))
    attn = ("y", "z", "core")
    every = ("y", "z", "core", "x")
    in_specs = (
        P(every, None),
        P(),
        P(every, None),
        P(every, None),
        P(),
        P(attn, "x", None),
        P(attn, "x", None),
        P(attn, None, "x"),
    )
    return jax.shard_map(shards, mesh=fine, in_specs=in_specs, out_specs=P(every, None), check_vma=False)
```

```python
import functools

import jax
import jax.numpy as jnp
from jax import lax
from jax.experimental import pallas as pl
from jax.experimental.pallas import tpu as pltpu
from jax.sharding import PartitionSpec as P

ROUTE_SCALE = 2.5
EPSILON = 1e-06
PAD = 128
RING = 4


def move(value, step):
    return lax.ppermute(value, "exp", [(i, (i + step) % RING) for i in range(RING)])


def direct(chunks):
    return [chunks[0], move(chunks[3], -1), move(chunks[2], 2), move(chunks[1], 1)]


def swap(value):
    return lax.all_to_all(value, "attn", split_axis=0, concat_axis=0, tiled=True)


def add(one, other):
    return (one.astype(jnp.float32) + other.astype(jnp.float32)).astype(jnp.bfloat16)


def prepare_kernel(place_ref, hidden_ref, gain_ref, routes_ref, scores_ref, capacity_ref, *out_refs):
    rows, top = routes_ref.shape
    experts = capacity_ref.shape[1]
    width = out_refs[0].shape[1] - PAD
    hidden = hidden_ref[...].astype(jnp.float32)
    scale = lax.rsqrt(jnp.mean(hidden * hidden, axis=1, keepdims=True) + EPSILON)
    routes = routes_ref[...]
    scores = scores_ref[...]
    weights = ROUTE_SCALE * scores / jnp.sum(scores, axis=1, keepdims=True)
    lane = lax.broadcasted_iota(jnp.int32, (rows, PAD), 1)
    named = lax.rem(lane, experts)
    match = jnp.zeros((rows, PAD), jnp.float32)
    weight = jnp.zeros((rows, PAD), jnp.float32)
    for k in range(top):
        same = routes[:, k : k + 1] == named
        match = jnp.where(same, 1.0, match)
        weight = jnp.where(same, weights[:, k : k + 1], weight)
    row = lax.broadcasted_iota(jnp.int32, (rows, PAD), 0)
    rank = jnp.zeros((rows, PAD), jnp.float32)
    for j in range(rows):
        later = (row > j) & (row < (j // 4 + 1) * 4)
        rank = rank + jnp.where(later, match[j : j + 1, :], 0.0)
    spread = (
        lax.broadcasted_iota(jnp.int32, (experts, PAD), 0)
        == lax.rem(lax.broadcasted_iota(jnp.int32, (experts, PAD), 1), experts)
    ).astype(jnp.float32)
    limit = jnp.broadcast_to(capacity_ref[...].astype(jnp.float32), (8, experts))
    limit = jnp.dot(limit, spread, preferred_element_type=jnp.float32)[0:1]
    kept = (match > 0.0) & (rank < limit)
    high = weight.astype(jnp.bfloat16).astype(jnp.float32)
    group = lane // experts
    value = jnp.where(group == 0, rank + 1.0, jnp.where(group == 1, high, weight - high))
    columns = jnp.where(kept & (group < 3), value, 0.0).astype(jnp.bfloat16)
    for r in range(RING):
        start = pl.multiple_of(lax.rem(place_ref[0] + r, RING) * width, PAD)
        part = hidden_ref[:, pl.ds(start, width)].astype(jnp.float32) * scale * gain_ref[:, pl.ds(start, width)]
        out_refs[r][:, :width] = part.astype(jnp.bfloat16)
        out_refs[r][:, width:] = columns


def finish_kernel(place_ref, hidden_ref, *refs):
    out_ref = refs[-1]
    width = refs[0].shape[1]
    for r in range(RING):
        start = pl.multiple_of(lax.rem(place_ref[0] + r, RING) * width, PAD)
        total = hidden_ref[:, pl.ds(start, width)].astype(jnp.float32) + refs[r][...].astype(jnp.float32)
        out_ref[:, pl.ds(start, width)] = total.astype(jnp.bfloat16)


def specs(count):
    return [pl.BlockSpec(memory_space=pltpu.SMEM)] + [pl.BlockSpec(memory_space=pltpu.VMEM)] * count


def pick_kernel(place_ref, *refs):
    lines = jnp.concatenate([ref[...].astype(jnp.float32) for ref in refs[:RING]], axis=0).astype(jnp.bfloat16)
    rows, width = lines.shape[0], lines.shape[1] - PAD
    for micro in range(2):
        out_ref = refs[RING + micro]
        slots = out_ref.shape[0]
        slot = lax.broadcasted_iota(jnp.int32, (slots, PAD), 0)
        lane = lax.broadcasted_iota(jnp.int32, (slots, PAD), 1)
        code = lax.dot_general(
            (lane == slot // 8).astype(jnp.bfloat16),
            lines[:, width:],
            (((1,), (1,)), ((), ())),
            preferred_element_type=jnp.float32,
        )
        slot = lax.broadcasted_iota(jnp.int32, (slots, rows), 0)
        row = lax.broadcasted_iota(jnp.int32, (slots, rows), 1)
        here = (lax.rem(slot, 8) // 2 == lax.rem(row // 8 + place_ref[0], RING)) & (lax.rem(row, 8) // 4 == micro)
        chosen = here & (code.astype(jnp.int32) == lax.rem(slot, 2) + 1)
        chosen = chosen.astype(jnp.float32).astype(jnp.bfloat16)
        out_ref[...] = jnp.dot(chosen, lines[:, :width], preferred_element_type=jnp.float32).astype(jnp.bfloat16)


def combine_kernel(experts, place_ref, *refs):
    lines = jnp.concatenate([ref[...].astype(jnp.float32) for ref in refs[:RING]], axis=0).astype(jnp.bfloat16)
    rows = lines.shape[0]
    total = jnp.zeros((rows, refs[-1].shape[1]), jnp.float32)
    for micro in range(2):
        returned = refs[RING + micro][...]
        slots = returned.shape[0]
        slot = lax.broadcasted_iota(jnp.int32, (slots, PAD), 0)
        lane = lax.broadcasted_iota(jnp.int32, (slots, PAD), 1)
        parts = [
            lax.dot_general(
                lines,
                (lane == slot // 8 + k * experts).astype(jnp.bfloat16),
                (((1,), (1,)), ((), ())),
                preferred_element_type=jnp.float32,
            )
            for k in range(3)
        ]
        row = lax.broadcasted_iota(jnp.int32, (rows, slots), 0)
        slot = lax.broadcasted_iota(jnp.int32, (rows, slots), 1)
        here = (lax.rem(slot, 8) // 2 == lax.rem(row // 8 + place_ref[0], RING)) & (lax.rem(row, 8) // 4 == micro)
        chosen = here & (parts[0].astype(jnp.int32) == lax.rem(slot, 2) + 1)
        for part in parts[1:]:
            weight = jnp.where(chosen, part, 0.0).astype(jnp.bfloat16)
            total += jnp.dot(weight, returned, preferred_element_type=jnp.float32)
    for r in range(RING):
        refs[RING + 2 + r][...] = total[r * rows // RING : (r + 1) * rows // RING].astype(jnp.bfloat16)


def shards(hidden, norm_gain, routes, route_scores, capacity, w_gate, w_up, w_down):
    experts = capacity.shape[0]
    place = lax.axis_index("exp").astype(jnp.int32)
    where = place.reshape(1)
    width, ff = w_gate.shape[1:]
    rows = hidden.shape[0]
    slots = experts * 8
    vmem = pl.BlockSpec(memory_space=pltpu.VMEM)
    blocks = pl.pallas_call(
        prepare_kernel,
        out_shape=[jax.ShapeDtypeStruct((rows, width + PAD), jnp.bfloat16)] * RING,
        in_specs=specs(5),
        out_specs=[vmem] * RING,
        name="prepare",
    )(where, hidden, norm_gain.reshape(1, -1), routes, route_scores, capacity.reshape(1, -1))
    mixed = direct(blocks)
    picked = pl.pallas_call(
        pick_kernel,
        out_shape=[jax.ShapeDtypeStruct((slots, width), jnp.bfloat16)] * 2,
        in_specs=specs(RING),
        out_specs=[vmem] * 2,
        name="pick",
    )(where, *mixed)
    entering = [swap(value.reshape(experts, 8, width)).reshape(slots, width) for value in picked]
    returned = []
    for value in entering:
        gate = jnp.dot(value, w_gate[0], preferred_element_type=jnp.float32).astype(jnp.bfloat16)
        up = jnp.dot(value, w_up[0], preferred_element_type=jnp.float32).astype(jnp.bfloat16)
        part = slots // RING
        half = part // 2
        own = [lax.rem(place + r, RING) * part for r in range(RING)]
        gate = [lax.dynamic_slice_in_dim(gate, start, part, axis=0) for start in own]
        up = [lax.dynamic_slice_in_dim(up, start, part, axis=0) for start in own]
        gate_far = move(gate[2], 1)
        up_far = move(up[2], -1)
        up_low = move(up[1], 1)
        gate_high = move(gate[3], -1)
        gate_low = move(add(gate[1], gate_far), 1)
        up_high = move(add(up[3], up_far), -1)
        gate_sum = gate[0].astype(jnp.float32) + gate_low.astype(jnp.float32) + gate_high.astype(jnp.float32)
        up_sum = up[0].astype(jnp.float32) + up_low.astype(jnp.float32) + up_high.astype(jnp.float32)
        activation = (jax.nn.silu(gate_sum) * up_sum).astype(jnp.bfloat16)
        low = move(activation, 1)
        high = move(activation, -1)
        far_low = move(low[:half], 1)
        far_high = move(high[half:], -1)
        whole = jnp.zeros((slots, ff), jnp.bfloat16)
        for piece, start in (
            (activation, own[0]), (high, own[1]), (far_low, own[2]), (far_high, own[2] + half), (low, own[3])
        ):
            whole = lax.dynamic_update_slice_in_dim(whole, piece, start, axis=0)
        expert_out = jnp.dot(whole, w_down[0], preferred_element_type=jnp.float32).astype(jnp.bfloat16)
        returned.append(swap(expert_out.reshape(experts, 8, width)).reshape(slots, width))
    sums = pl.pallas_call(
        functools.partial(combine_kernel, experts),
        out_shape=[jax.ShapeDtypeStruct((rows, width), jnp.bfloat16)] * RING,
        in_specs=specs(RING + 2),
        out_specs=[vmem] * RING,
        name="combine",
    )(where, *[value[:, width:] for value in mixed], *returned)
    back = direct(sums)
    return pl.pallas_call(
        finish_kernel,
        out_shape=jax.ShapeDtypeStruct(hidden.shape, jnp.bfloat16),
        in_specs=specs(1 + RING),
        out_specs=vmem,
        name="finish",
    )(where, hidden, *back)


def solution(mesh):
    in_specs = (
        P(("attn", "exp"), None),
        P(),
        P(("attn", "exp"), None),
        P(("attn", "exp"), None),
        P(),
        P("attn", "exp", None),
        P("attn", "exp", None),
        P("attn", None, "exp"),
    )
    out_specs = P(("attn", "exp"), None)
    return jax.shard_map(shards, mesh=mesh, in_specs=in_specs, out_specs=out_specs, check_vma=False)
```

```python
import jax
import jax.numpy as jnp
from jax import lax
from jax.experimental import pallas as pl
from jax.experimental.pallas import tpu as pltpu
from jax.sharding import PartitionSpec as P

ROUTE_SCALE = 2.5
EPSILON = 1e-06
PAD = 128
RING = 4


def attn_pairs(stage, step):
    pairs = []
    for y in range(RING):
        for z in range(RING):
            for core in range(2):
                to = [y, z, core]
                if stage == "core":
                    to[2] = 1 - core
                else:
                    axis = stage if core == 0 else 1 - stage
                    to[axis] = (to[axis] + step) % RING
                pairs.append(((y * RING + z) * 2 + core, (to[0] * RING + to[1]) * 2 + to[2]))
    return pairs


def move(value, axis, step):
    if axis == "x":
        return lax.ppermute(value, "exp", [(i, (i + step) % RING) for i in range(RING)])
    return lax.ppermute(value, "attn", attn_pairs(axis, step))


def direct(chunks, axis):
    return [chunks[0], move(chunks[3], axis, -1), move(chunks[2], axis, 2), move(chunks[1], axis, 1)]


def gather_ring(value, axis):
    half = value.shape[0] // 2
    low = move(value, axis, 1)
    high = move(value, axis, -1)
    first = move(low[:half], axis, 1)
    second = move(high[half:], axis, -1)
    return [value, high, first, second, low]


def add(one, other):
    return (one.astype(jnp.float32) + other.astype(jnp.float32)).astype(jnp.bfloat16)


def scatter_ring(chunks, axis):
    half = chunks[2].shape[0] // 2
    first = move(chunks[2][:half], axis, 1)
    second = move(chunks[2][half:], axis, -1)
    up = jnp.concatenate([add(chunks[1][:half], first), chunks[1][half:]], axis=0)
    down = jnp.concatenate([chunks[3][:half], add(chunks[3][half:], second)], axis=0)
    low = move(up, axis, 1)
    high = move(down, axis, -1)
    total = chunks[0].astype(jnp.float32) + low.astype(jnp.float32) + high.astype(jnp.float32)
    return total.astype(jnp.bfloat16)


def prepare_kernel(place_ref, hidden_ref, gain_ref, routes_ref, scores_ref, capacity_ref, *out_refs):
    rows, top = routes_ref.shape
    experts = capacity_ref.shape[1]
    width = out_refs[0].shape[1] - PAD
    hidden = hidden_ref[...].astype(jnp.float32)
    scale = lax.rsqrt(jnp.mean(hidden * hidden, axis=1, keepdims=True) + EPSILON)
    routes = routes_ref[...]
    scores = scores_ref[...]
    weights = ROUTE_SCALE * scores / jnp.sum(scores, axis=1, keepdims=True)
    lane = lax.broadcasted_iota(jnp.int32, (rows, PAD), 1)
    named = lax.rem(lane, experts)
    match = jnp.zeros((rows, PAD), jnp.float32)
    weight = jnp.zeros((rows, PAD), jnp.float32)
    for k in range(top):
        same = routes[:, k : k + 1] == named
        match = jnp.where(same, 1.0, match)
        weight = jnp.where(same, weights[:, k : k + 1], weight)
    row = lax.broadcasted_iota(jnp.int32, (rows, PAD), 0)
    rank = jnp.zeros((rows, PAD), jnp.float32)
    for j in range(rows):
        later = (row > j) & (row < (j // 4 + 1) * 4)
        rank = rank + jnp.where(later, match[j : j + 1, :], 0.0)
    spread = (
        lax.broadcasted_iota(jnp.int32, (experts, PAD), 0)
        == lax.rem(lax.broadcasted_iota(jnp.int32, (experts, PAD), 1), experts)
    ).astype(jnp.float32)
    limit = jnp.broadcast_to(capacity_ref[...].astype(jnp.float32), (8, experts))
    limit = jnp.dot(limit, spread, preferred_element_type=jnp.float32)[0:1]
    kept = (match > 0.0) & (rank < limit)
    high = weight.astype(jnp.bfloat16).astype(jnp.float32)
    group = lane // experts
    value = jnp.where(group == 0, rank + 1.0, jnp.where(group == 1, high, weight - high))
    columns = jnp.where(kept & (group < 3), value, 0.0).astype(jnp.bfloat16)
    for r in range(RING):
        start = pl.multiple_of(lax.rem(place_ref[0] + r, RING) * width, PAD)
        part = hidden_ref[:, pl.ds(start, width)].astype(jnp.float32) * scale * gain_ref[:, pl.ds(start, width)]
        out_refs[r][:, :width] = part.astype(jnp.bfloat16)
        out_refs[r][:, width:] = columns


def finish_kernel(place_ref, hidden_ref, *refs):
    out_ref = refs[-1]
    width = refs[0].shape[1]
    for r in range(RING):
        start = pl.multiple_of(lax.rem(place_ref[0] + r, RING) * width, PAD)
        total = hidden_ref[:, pl.ds(start, width)].astype(jnp.float32) + refs[r][...].astype(jnp.float32)
        out_ref[:, pl.ds(start, width)] = total.astype(jnp.bfloat16)


def join_kernel(*refs):
    refs[-1][...] = jnp.concatenate([ref[...].astype(jnp.float32) for ref in refs[:-1]], axis=0).astype(jnp.bfloat16)


def join(pieces):
    vmem = pl.BlockSpec(memory_space=pltpu.VMEM)
    rows = sum(piece.shape[0] for piece in pieces)
    return pl.pallas_call(
        join_kernel,
        out_shape=jax.ShapeDtypeStruct((rows, pieces[0].shape[1]), jnp.bfloat16),
        in_specs=[vmem] * len(pieces),
        out_specs=vmem,
        name="join",
    )(*pieces)


def specs(count):
    return [pl.BlockSpec(memory_space=pltpu.SMEM)] + [pl.BlockSpec(memory_space=pltpu.VMEM)] * count


def choose(picks, expert):
    lanes = jnp.arange(PAD)[None, :]
    code = jnp.sum(jnp.where(lanes == expert, picks, 0.0), axis=1)
    rows = picks.shape[0]
    per = rows // 16
    row = jnp.arange(rows, dtype=jnp.int32)
    slot = jnp.arange(rows // 2, dtype=jnp.int32)
    block = row % 32 // 8 * per + row // 32 * 2 + row % 8 // 4
    chosen = (block[:, None] == slot[None, :] // 2) & (
        code.astype(jnp.int32)[:, None] == (slot % 2 + 1)[None, :]
    )
    return chosen.astype(jnp.bfloat16)


def pick(chosen, rows):
    return lax.dot_general(
        chosen, rows, (((0,), (0,)), ((), ())), preferred_element_type=jnp.float32
    ).astype(jnp.bfloat16)


def shards(hidden, norm_gain, routes, route_scores, capacity, w_gate, w_up, w_down):
    experts = capacity.shape[0]
    expert = lax.axis_index("attn")
    other = expert + 1 - 2 * (expert % 2)
    place = lax.axis_index("exp").astype(jnp.int32).reshape(1)
    width = w_gate.shape[1]
    rows = hidden.shape[0]
    blocks = pl.pallas_call(
        prepare_kernel,
        out_shape=[jax.ShapeDtypeStruct((rows, width + PAD), jnp.bfloat16)] * RING,
        in_specs=specs(5),
        out_specs=[pl.BlockSpec(memory_space=pltpu.VMEM)] * RING,
        name="prepare",
    )(place, hidden, norm_gain.reshape(1, -1), routes, route_scores, capacity.reshape(1, -1))
    lines = join(direct(blocks, "x"))
    lines = join(direct([lines] * RING, 0))
    lines = jnp.concatenate(gather_ring(lines, 1), axis=0)
    picks = lines[:, width:].astype(jnp.float32)
    chosen_own = choose(picks, expert)
    chosen_other = choose(picks, other)
    picked = [move(pick(chosen_other, lines), "core", 1), pick(chosen_own, lines)]
    lane = jnp.arange(PAD)[None, :]
    mine = (lane == expert + experts) | (lane == expert + 2 * experts)
    parts, scales = [], []
    for chunk in range(2):
        slots = picked[chunk]
        if chunk == 1:
            slots, *parts[0][0:2] = lax.optimization_barrier((slots, *parts[0][0:2]))
        scales.append(jnp.sum(jnp.where(mine, slots[:, width:].astype(jnp.float32), 0.0), axis=1))
        slots = slots[:, :width]
        gate = jnp.dot(slots, w_gate[0], preferred_element_type=jnp.float32).astype(jnp.bfloat16)
        up = jnp.dot(slots, w_up[0], preferred_element_type=jnp.float32).astype(jnp.bfloat16)
        part = slots.shape[0] // RING
        gate = [gate[r * part : (r + 1) * part] for r in range(RING)]
        up = [up[r * part : (r + 1) * part] for r in range(RING)]
        gate_far = move(gate[2], "x", 1)
        up_far = move(up[2], "x", -1)
        up_low = move(up[1], "x", 1)
        gate_high = move(gate[3], "x", -1)
        parts.append([gate_far, up_far, up_low, gate_high, gate, up])
    out = []
    for chunk in range(2):
        gate_far, up_far, up_low, gate_high, gate, up = parts[chunk]
        gate_low = move(add(gate[1], gate_far), "x", 1)
        up_high = move(add(up[3], up_far), "x", -1)
        if chunk == 0:
            gate_low, parts[1][4][0] = lax.optimization_barrier((gate_low, parts[1][4][0]))
            up_high, parts[1][5][0] = lax.optimization_barrier((up_high, parts[1][5][0]))
        gate_sum = gate[0].astype(jnp.float32) + gate_low.astype(jnp.float32) + gate_high.astype(jnp.float32)
        up_sum = up[0].astype(jnp.float32) + up_low.astype(jnp.float32) + up_high.astype(jnp.float32)
        activation = (jax.nn.silu(gate_sum) * up_sum).astype(jnp.bfloat16)
        activation = jnp.concatenate(gather_ring(activation, "x"), axis=0)
        expert_out = jnp.dot(activation, w_down[0], preferred_element_type=jnp.float32)
        expert_out = (expert_out * scales[chunk][:, None]).astype(jnp.bfloat16)
        out.append(move(expert_out, "core", 1) if chunk == 0 else expert_out)
    returned = jnp.concatenate(out, axis=0)
    chosen = jnp.concatenate([chosen_other, chosen_own], axis=1)
    summed = jnp.dot(chosen, returned, preferred_element_type=jnp.float32).astype(jnp.bfloat16)
    part = summed.shape[0] // RING
    summed = scatter_ring([summed[r * part : (r + 1) * part] for r in range(RING)], 1)
    part = part // RING
    pieces = direct([summed[r * part : (r + 1) * part] for r in range(RING)], 0)
    summed = sum(piece.astype(jnp.float32) for piece in pieces).astype(jnp.bfloat16)
    back = direct([summed[r * rows : (r + 1) * rows] for r in range(RING)], "x")
    return pl.pallas_call(
        finish_kernel,
        out_shape=jax.ShapeDtypeStruct(hidden.shape, jnp.bfloat16),
        in_specs=specs(1 + RING),
        out_specs=pl.BlockSpec(memory_space=pltpu.VMEM),
        name="finish",
    )(place, hidden, *back)


def solution(mesh):
    in_specs = (
        P(("attn", "exp"), None),
        P(),
        P(("attn", "exp"), None),
        P(("attn", "exp"), None),
        P(),
        P("attn", "exp", None),
        P("attn", "exp", None),
        P("attn", None, "exp"),
    )
    out_specs = P(("attn", "exp"), None)
    return jax.shard_map(shards, mesh=mesh, in_specs=in_specs, out_specs=out_specs, check_vma=False)
```

```python
import jax
import jax.numpy as jnp
from jax import lax
from jax.experimental import pallas as pl
from jax.experimental.pallas import tpu as pltpu
from jax.sharding import PartitionSpec as P

ROUTE_SCALE = 2.5
EPSILON = 1e-06
PAD = 128
RING = 4


def attn_pairs(stage, step):
    pairs = []
    for y in range(RING):
        for z in range(RING):
            for core in range(2):
                to = [y, z, core]
                if stage == "core":
                    to[2] = 1 - core
                else:
                    axis = stage if core == 0 else 1 - stage
                    to[axis] = (to[axis] + step) % RING
                pairs.append(((y * RING + z) * 2 + core, (to[0] * RING + to[1]) * 2 + to[2]))
    return pairs


def move(value, axis, step):
    if axis == "x":
        return lax.ppermute(value, "exp", [(i, (i + step) % RING) for i in range(RING)])
    return lax.ppermute(value, "attn", attn_pairs(axis, step))


def direct(chunks, axis):
    return [chunks[0], move(chunks[3], axis, -1), move(chunks[2], axis, 2), move(chunks[1], axis, 1)]


def gather_ring(value, axis):
    half = value.shape[0] // 2
    low = move(value, axis, 1)
    high = move(value, axis, -1)
    first = move(low[:half], axis, 1)
    second = move(high[half:], axis, -1)
    return [value, high, first, second, low]


def add(one, other):
    return (one.astype(jnp.float32) + other.astype(jnp.float32)).astype(jnp.bfloat16)


def scatter_ring(own, chunks, axis):
    half = chunks[1].shape[0] // 2
    first = move(chunks[1][:half], axis, 1)
    second = move(chunks[1][half:], axis, -1)
    up = jnp.concatenate([add(chunks[0][:half], first), chunks[0][half:]], axis=0)
    down = jnp.concatenate([chunks[2][:half], add(chunks[2][half:], second)], axis=0)
    low = move(up, axis, 1)
    high = move(down, axis, -1)
    total = own.astype(jnp.float32) + low.astype(jnp.float32) + high.astype(jnp.float32)
    return total.astype(jnp.bfloat16)


def prepare_kernel(place_ref, hidden_ref, gain_ref, routes_ref, scores_ref, capacity_ref, *out_refs):
    rows, top = routes_ref.shape
    experts = capacity_ref.shape[1]
    width = out_refs[0].shape[1] - PAD
    hidden = hidden_ref[...].astype(jnp.float32)
    scale = lax.rsqrt(jnp.mean(hidden * hidden, axis=1, keepdims=True) + EPSILON)
    routes = routes_ref[...]
    scores = scores_ref[...]
    weights = ROUTE_SCALE * scores / jnp.sum(scores, axis=1, keepdims=True)
    lane = lax.broadcasted_iota(jnp.int32, (rows, PAD), 1)
    named = lax.rem(lane, experts)
    match = jnp.zeros((rows, PAD), jnp.float32)
    weight = jnp.zeros((rows, PAD), jnp.float32)
    for k in range(top):
        same = routes[:, k : k + 1] == named
        match = jnp.where(same, 1.0, match)
        weight = jnp.where(same, weights[:, k : k + 1], weight)
    row = lax.broadcasted_iota(jnp.int32, (rows, PAD), 0)
    rank = jnp.zeros((rows, PAD), jnp.float32)
    for j in range(rows):
        later = (row > j) & (row < (j // 4 + 1) * 4)
        rank = rank + jnp.where(later, match[j : j + 1, :], 0.0)
    spread = (
        lax.broadcasted_iota(jnp.int32, (experts, PAD), 0)
        == lax.rem(lax.broadcasted_iota(jnp.int32, (experts, PAD), 1), experts)
    ).astype(jnp.float32)
    limit = jnp.broadcast_to(capacity_ref[...].astype(jnp.float32), (8, experts))
    limit = jnp.dot(limit, spread, preferred_element_type=jnp.float32)[0:1]
    kept = (match > 0.0) & (rank < limit)
    high = weight.astype(jnp.bfloat16).astype(jnp.float32)
    group = lane // experts
    value = jnp.where(group == 0, rank + 1.0, jnp.where(group == 1, high, weight - high))
    columns = jnp.where(kept & (group < 3), value, 0.0).astype(jnp.bfloat16)
    for r in range(RING):
        start = pl.multiple_of(lax.rem(place_ref[0] + r, RING) * width, PAD)
        part = hidden_ref[:, pl.ds(start, width)].astype(jnp.float32) * scale * gain_ref[:, pl.ds(start, width)]
        out_refs[r][:, :width] = part.astype(jnp.bfloat16)
        out_refs[r][:, width:] = columns


def finish_kernel(place_ref, hidden_ref, *refs):
    out_ref = refs[-1]
    width = refs[0].shape[1]
    for r in range(RING):
        start = pl.multiple_of(lax.rem(place_ref[0] + r, RING) * width, PAD)
        total = hidden_ref[:, pl.ds(start, width)].astype(jnp.float32) + refs[r][...].astype(jnp.float32)
        out_ref[:, pl.ds(start, width)] = total.astype(jnp.bfloat16)


def specs(count):
    return [pl.BlockSpec(memory_space=pltpu.SMEM)] + [pl.BlockSpec(memory_space=pltpu.VMEM)] * count


def choose(picks, expert):
    lanes = jnp.arange(PAD)[None, :]
    code = jnp.sum(jnp.where(lanes == expert, picks, 0.0), axis=1)
    rows = picks.shape[0]
    per = rows // 16
    row = jnp.arange(rows, dtype=jnp.int32)
    slot = jnp.arange(rows // 2, dtype=jnp.int32)
    block = row % 32 // 8 * per + row // 32 * 2 + row % 8 // 4
    chosen = (block[:, None] == slot[None, :] // 2) & (
        code.astype(jnp.int32)[:, None] == (slot % 2 + 1)[None, :]
    )
    return chosen.astype(jnp.bfloat16)


def pick(chosen, rows):
    return lax.dot_general(
        chosen, rows, (((0,), (0,)), ((), ())), preferred_element_type=jnp.float32
    ).astype(jnp.bfloat16)


def shards(hidden, norm_gain, routes, route_scores, capacity, w_gate, w_up, w_down):
    experts = capacity.shape[0]
    expert = lax.axis_index("attn")
    other = expert + 1 - 2 * (expert % 2)
    place = lax.axis_index("exp").astype(jnp.int32).reshape(1)
    width = w_gate.shape[1]
    rows = hidden.shape[0]
    blocks = pl.pallas_call(
        prepare_kernel,
        out_shape=[jax.ShapeDtypeStruct((rows, width + PAD), jnp.bfloat16)] * RING,
        in_specs=specs(5),
        out_specs=[pl.BlockSpec(memory_space=pltpu.VMEM)] * RING,
        name="prepare",
    )(place, hidden, norm_gain.reshape(1, -1), routes, route_scores, capacity.reshape(1, -1))
    lines = jnp.concatenate(direct(blocks, "x"), axis=0)
    near = jnp.concatenate(direct([lines] * RING, 0), axis=0)
    far = jnp.concatenate(gather_ring(near, 1)[1:], axis=0)
    lane = jnp.arange(PAD)[None, :]
    mine = (lane == expert + experts) | (lane == expert + 2 * experts)
    spread = []
    after = None
    for lines in (near, far):
        picks = lines[:, width:].astype(jnp.float32)
        chosen = [choose(picks, expert), choose(picks, other)]
        quarter = lines.shape[0] // 2 // RING
        theirs = move(pick(chosen[1], lines), "core", 1)
        slots = [value.reshape(RING, quarter, width + PAD) for value in (pick(chosen[0], lines), theirs)]
        slots = jnp.concatenate(slots, axis=1).reshape(RING * 2 * quarter, width + PAD)
        scale = jnp.sum(jnp.where(mine, slots[:, width:].astype(jnp.float32), 0.0), axis=1)
        slots = slots[:, :width]
        if after is not None:
            slots, after = lax.optimization_barrier((slots, after))
        part = 2 * quarter
        gate = jnp.dot(slots, w_gate[0], preferred_element_type=jnp.float32).astype(jnp.bfloat16)
        gate = [gate[r * part : (r + 1) * part] for r in range(RING)]
        gate_far = move(gate[2], "x", 1)
        gate_high = move(gate[3], "x", -1)
        up = jnp.dot(slots, w_up[0], preferred_element_type=jnp.float32).astype(jnp.bfloat16)
        up = [up[r * part : (r + 1) * part] for r in range(RING)]
        up_far = move(up[2], "x", -1)
        up_low = move(up[1], "x", 1)
        gate_low = move(add(gate[1], gate_far), "x", 1)
        up_high = move(add(up[3], up_far), "x", -1)
        if after is not None:
            whole = jnp.concatenate(gather_ring(after, "x"), axis=0)
            gate_low, whole = lax.optimization_barrier((gate_low, whole))
            near_state[0] = whole
        gate_sum = gate[0].astype(jnp.float32) + gate_low.astype(jnp.float32) + gate_high.astype(jnp.float32)
        up_sum = up[0].astype(jnp.float32) + up_low.astype(jnp.float32) + up_high.astype(jnp.float32)
        activation = (jax.nn.silu(gate_sum) * up_sum).astype(jnp.bfloat16)
        if after is None:
            after = activation
            near_state = [None, scale, jnp.concatenate(chosen, axis=1)]
    far_state = [jnp.concatenate(gather_ring(activation, "x"), axis=0), scale, jnp.concatenate(chosen, axis=1)]
    for whole, scale, chosen in (near_state, far_state):
        if spread:
            whole, spread[0] = lax.optimization_barrier((whole, spread[0]))
        expert_out = jnp.dot(whole, w_down[0], preferred_element_type=jnp.float32)
        expert_out = (expert_out * scale[:, None]).astype(jnp.bfloat16)
        expert_out = expert_out.reshape(RING, 2, -1, width)
        theirs = move(expert_out[:, 1].reshape(-1, width), "core", 1)
        returned = jnp.concatenate([expert_out[:, 0].reshape(-1, width), theirs], axis=0)
        spread.append(jnp.dot(chosen, returned, preferred_element_type=jnp.float32).astype(jnp.bfloat16))
    part = spread[0].shape[0]
    summed = scatter_ring(spread[0], [spread[1][r * part : (r + 1) * part] for r in range(RING - 1)], 1)
    part = part // RING
    pieces = direct([summed[r * part : (r + 1) * part] for r in range(RING)], 0)
    summed = sum(piece.astype(jnp.float32) for piece in pieces).astype(jnp.bfloat16)
    back = direct([summed[r * rows : (r + 1) * rows] for r in range(RING)], "x")
    return pl.pallas_call(
        finish_kernel,
        out_shape=jax.ShapeDtypeStruct(hidden.shape, jnp.bfloat16),
        in_specs=specs(1 + RING),
        out_specs=pl.BlockSpec(memory_space=pltpu.VMEM),
        name="finish",
    )(place, hidden, *back)


def solution(mesh):
    in_specs = (
        P(("attn", "exp"), None),
        P(),
        P(("attn", "exp"), None),
        P(("attn", "exp"), None),
        P(),
        P("attn", "exp", None),
        P("attn", "exp", None),
        P("attn", None, "exp"),
    )
    out_specs = P(("attn", "exp"), None)
    return jax.shard_map(shards, mesh=mesh, in_specs=in_specs, out_specs=out_specs, check_vma=False)
```

```python
import jax
import jax.numpy as jnp
from jax import lax
from jax.experimental import pallas as pl
from jax.experimental.pallas import tpu as pltpu
from jax.sharding import PartitionSpec as P

ROUTE_SCALE = 2.5
EPSILON = 1e-06
PAD = 128
RING = 4


def attn_pairs(stage, step):
    pairs = []
    for y in range(RING):
        for z in range(RING):
            for core in range(2):
                to = [y, z, core]
                if stage == "core":
                    to[2] = 1 - core
                else:
                    axis = stage if core == 0 else 1 - stage
                    to[axis] = (to[axis] + step) % RING
                pairs.append(((y * RING + z) * 2 + core, (to[0] * RING + to[1]) * 2 + to[2]))
    return pairs


def move(value, axis, step):
    if axis == "x":
        return lax.ppermute(value, "exp", [(i, (i + step) % RING) for i in range(RING)])
    return lax.ppermute(value, "attn", attn_pairs(axis, step))


def direct(chunks, axis):
    return [chunks[0], move(chunks[3], axis, -1), move(chunks[2], axis, 2), move(chunks[1], axis, 1)]


def gather_ring(value, axis):
    half = value.shape[0] // 2
    low = move(value, axis, 1)
    high = move(value, axis, -1)
    first = move(low[:half], axis, 1)
    second = move(high[half:], axis, -1)
    return [value, high, first, second, low]


def add(one, other):
    return (one.astype(jnp.float32) + other.astype(jnp.float32)).astype(jnp.bfloat16)


def scatter_ring(own, chunks, axis):
    half = chunks[1].shape[0] // 2
    first = move(chunks[1][:half], axis, 1)
    second = move(chunks[1][half:], axis, -1)
    up = jnp.concatenate([add(chunks[0][:half], first), chunks[0][half:]], axis=0)
    down = jnp.concatenate([chunks[2][:half], add(chunks[2][half:], second)], axis=0)
    low = move(up, axis, 1)
    high = move(down, axis, -1)
    total = own.astype(jnp.float32) + low.astype(jnp.float32) + high.astype(jnp.float32)
    return total.astype(jnp.bfloat16)


def prepare_kernel(place_ref, hidden_ref, gain_ref, routes_ref, scores_ref, capacity_ref, *out_refs):
    rows, top = routes_ref.shape
    experts = capacity_ref.shape[1]
    width = out_refs[0].shape[1] - PAD
    hidden = hidden_ref[...].astype(jnp.float32)
    scale = lax.rsqrt(jnp.mean(hidden * hidden, axis=1, keepdims=True) + EPSILON)
    routes = routes_ref[...]
    scores = scores_ref[...]
    weights = ROUTE_SCALE * scores / jnp.sum(scores, axis=1, keepdims=True)
    lane = lax.broadcasted_iota(jnp.int32, (rows, PAD), 1)
    named = lax.rem(lane, experts)
    match = jnp.zeros((rows, PAD), jnp.float32)
    weight = jnp.zeros((rows, PAD), jnp.float32)
    for k in range(top):
        same = routes[:, k : k + 1] == named
        match = jnp.where(same, 1.0, match)
        weight = jnp.where(same, weights[:, k : k + 1], weight)
    row = lax.broadcasted_iota(jnp.int32, (rows, PAD), 0)
    rank = jnp.zeros((rows, PAD), jnp.float32)
    for j in range(rows):
        later = (row > j) & (row < (j // 4 + 1) * 4)
        rank = rank + jnp.where(later, match[j : j + 1, :], 0.0)
    spread = (
        lax.broadcasted_iota(jnp.int32, (experts, PAD), 0)
        == lax.rem(lax.broadcasted_iota(jnp.int32, (experts, PAD), 1), experts)
    ).astype(jnp.float32)
    limit = jnp.broadcast_to(capacity_ref[...].astype(jnp.float32), (8, experts))
    limit = jnp.dot(limit, spread, preferred_element_type=jnp.float32)[0:1]
    kept = (match > 0.0) & (rank < limit)
    high = weight.astype(jnp.bfloat16).astype(jnp.float32)
    group = lane // experts
    value = jnp.where(group == 0, rank + 1.0, jnp.where(group == 1, high, weight - high))
    columns = jnp.where(kept & (group < 3), value, 0.0).astype(jnp.bfloat16)
    for r in range(RING):
        start = pl.multiple_of(lax.rem(place_ref[0] + r, RING) * width, PAD)
        part = hidden_ref[:, pl.ds(start, width)].astype(jnp.float32) * scale * gain_ref[:, pl.ds(start, width)]
        out_refs[r][:, :width] = part.astype(jnp.bfloat16)
        out_refs[r][:, width:] = columns


def finish_kernel(place_ref, hidden_ref, *refs):
    out_ref = refs[-1]
    width = refs[0].shape[1]
    for r in range(RING):
        start = pl.multiple_of(lax.rem(place_ref[0] + r, RING) * width, PAD)
        total = hidden_ref[:, pl.ds(start, width)].astype(jnp.float32) + refs[r][...].astype(jnp.float32)
        out_ref[:, pl.ds(start, width)] = total.astype(jnp.bfloat16)


def specs(count):
    return [pl.BlockSpec(memory_space=pltpu.SMEM)] + [pl.BlockSpec(memory_space=pltpu.VMEM)] * count


def choose(picks, expert):
    lanes = jnp.arange(PAD)[None, :]
    code = jnp.sum(jnp.where(lanes == expert, picks, 0.0), axis=1)
    rows = picks.shape[0]
    per = rows // 16
    row = jnp.arange(rows, dtype=jnp.int32)
    slot = jnp.arange(rows // 2, dtype=jnp.int32)
    block = row % 32 // 8 * per + row // 32 * 2 + row % 8 // 4
    chosen = (block[:, None] == slot[None, :] // 2) & (
        code.astype(jnp.int32)[:, None] == (slot % 2 + 1)[None, :]
    )
    return chosen.astype(jnp.bfloat16)


def pick(chosen, rows):
    return lax.dot_general(
        chosen, rows, (((0,), (0,)), ((), ())), preferred_element_type=jnp.float32
    ).astype(jnp.bfloat16)


def hold(first, then):
    count = len(first)
    values = lax.optimization_barrier((*first, *then))
    return values[:count], values[count:]


def shards(hidden, norm_gain, routes, route_scores, capacity, w_gate, w_up, w_down):
    experts = capacity.shape[0]
    expert = lax.axis_index("attn")
    other = expert + 1 - 2 * (expert % 2)
    place = lax.axis_index("exp").astype(jnp.int32).reshape(1)
    width = w_gate.shape[1]
    rows = hidden.shape[0]
    blocks = pl.pallas_call(
        prepare_kernel,
        out_shape=[jax.ShapeDtypeStruct((rows, width + PAD), jnp.bfloat16)] * RING,
        in_specs=specs(5),
        out_specs=[pl.BlockSpec(memory_space=pltpu.VMEM)] * RING,
        name="prepare",
    )(place, hidden, norm_gain.reshape(1, -1), routes, route_scores, capacity.reshape(1, -1))
    lane = jnp.arange(PAD)[None, :]
    mine = (lane == expert + experts) | (lane == expert + 2 * experts)

    def enter(lines, cuts):
        picks = lines[:, width:].astype(jnp.float32)
        quarter = lines.shape[0] // 2 // RING
        theirs = move(pick(choose(picks, other), lines), "core", 1)
        both = [value.reshape(RING, quarter, width + PAD) for value in (pick(choose(picks, expert), lines), theirs)]
        slots = [value[:, low:high] for low, high in zip(cuts, cuts[1:] + [quarter]) for value in both]
        slots = jnp.concatenate(slots, axis=1).reshape(RING * 2 * quarter, width + PAD)
        scale = jnp.sum(jnp.where(mine, slots[:, width:].astype(jnp.float32), 0.0), axis=1)
        return slots[:, :width], scale

    def product(slots, weights):
        part = slots.shape[0] // RING
        value = jnp.dot(slots, weights[0], preferred_element_type=jnp.float32).astype(jnp.bfloat16)
        return [value[r * part : (r + 1) * part] for r in range(RING)]

    def activate(gate, gate_low, gate_high, up, up_low, up_high):
        gate_sum = gate.astype(jnp.float32) + gate_low.astype(jnp.float32) + gate_high.astype(jnp.float32)
        up_sum = up.astype(jnp.float32) + up_low.astype(jnp.float32) + up_high.astype(jnp.float32)
        return (jax.nn.silu(gate_sum) * up_sum).astype(jnp.bfloat16)

    def leave(whole, scale, lines):
        picks = lines[:, width:].astype(jnp.float32)
        chosen = jnp.concatenate([choose(picks, expert), choose(picks, other)], axis=1)
        out = jnp.dot(whole, w_down[0], preferred_element_type=jnp.float32)
        out = (out * scale[:, None]).astype(jnp.bfloat16).reshape(RING, 2, -1, width)
        theirs = move(out[:, 1].reshape(-1, width), "core", 1)
        returned = jnp.concatenate([out[:, 0].reshape(-1, width), theirs], axis=0)
        return jnp.dot(chosen, returned, preferred_element_type=jnp.float32).astype(jnp.bfloat16)

    lines = jnp.concatenate(direct(blocks, "x"), axis=0)
    near = jnp.concatenate(direct([lines] * RING, 0), axis=0)
    low, high = move(near, 1, 1), move(near, 1, -1)
    slots, near_scale = enter(near, [0])
    gate, up = product(slots, w_gate), product(slots, w_up)
    (low, high), near_parts = hold((low, high), (*gate, *up))
    gate, up = near_parts[:RING], near_parts[RING:]
    half = near.shape[0] // 2
    first, second = move(low[:half], 1, 1), move(high[half:], 1, -1)
    gate_far, up_far = move(gate[2], "x", 1), move(up[2], "x", -1)
    up_low, gate_high = move(up[1], "x", 1), move(gate[3], "x", -1)
    (first, second), (gate_far, up_far) = hold((first, second), (gate_far, up_far))
    gate_low, up_high = move(add(gate[1], gate_far), "x", 1), move(add(up[3], up_far), "x", -1)
    near_act = activate(gate[0], gate_low, gate_high, up[0], up_low, up_high)
    two = jnp.concatenate([first, second], axis=0)
    one = jnp.concatenate([high, low], axis=0)
    far = jnp.concatenate([first, second, high, low], axis=0)
    cut = near.shape[0] // 2 // RING
    slots, far_scale = enter(far, [0, cut])
    gate = product(slots, w_gate)
    gate_far, gate_high = move(gate[2], "x", 1), move(gate[3], "x", -1)
    (near_act,), (slots,) = hold((near_act,), (slots,))
    near_low, near_high = move(near_act, "x", 1), move(near_act, "x", -1)
    up = product(slots, w_up)
    (near_low, near_high), up = hold((near_low, near_high), up)
    up_far, up_low = move(up[2], "x", -1), move(up[1], "x", 1)
    gate_low, up_high = move(add(gate[1], gate_far), "x", 1), move(add(up[3], up_far), "x", -1)
    (gate_high, up_low), (near_low, near_high) = hold((gate_high, up_low), (near_low, near_high))
    half = near_act.shape[0] // 2
    near_first, near_second = move(near_low[:half], "x", 1), move(near_high[half:], "x", -1)
    (gate_low, up_high), (near_first, near_second) = hold((gate_low, up_high), (near_first, near_second))
    near_whole = jnp.concatenate([near_act, near_high, near_first, near_second, near_low], axis=0)
    far_act = activate(gate[0], gate_low, gate_high, up[0], up_low, up_high)
    pieces = gather_ring(far_act, "x")
    near_sum = leave(near_whole, near_scale, near)
    (near_sum,), pieces = hold((near_sum,), pieces)
    inner = 2 * cut
    two_whole = jnp.concatenate([pieces[r][:inner] for r in (0, 1, 2, 4)], axis=0)
    one_whole = jnp.concatenate([pieces[0][inner:], pieces[1][inner:], pieces[2][inner:], pieces[3], pieces[4][inner:]], axis=0)
    far_scale = far_scale.reshape(RING, -1)
    two_sum = leave(two_whole, far_scale[:, :inner].reshape(-1), two)
    one_sum = leave(one_whole, far_scale[:, inner:].reshape(-1), one)
    part = near.shape[0]
    summed = scatter_ring(near_sum, [one_sum[:part], two_sum, one_sum[part:]], 1)
    part = part // RING
    pieces = direct([summed[r * part : (r + 1) * part] for r in range(RING)], 0)
    summed = sum(piece.astype(jnp.float32) for piece in pieces).astype(jnp.bfloat16)
    back = direct([summed[r * rows : (r + 1) * rows] for r in range(RING)], "x")
    return pl.pallas_call(
        finish_kernel,
        out_shape=jax.ShapeDtypeStruct(hidden.shape, jnp.bfloat16),
        in_specs=specs(1 + RING),
        out_specs=pl.BlockSpec(memory_space=pltpu.VMEM),
        name="finish",
    )(place, hidden, *back)


def solution(mesh):
    in_specs = (
        P(("attn", "exp"), None),
        P(),
        P(("attn", "exp"), None),
        P(("attn", "exp"), None),
        P(),
        P("attn", "exp", None),
        P("attn", "exp", None),
        P("attn", None, "exp"),
    )
    out_specs = P(("attn", "exp"), None)
    return jax.shard_map(shards, mesh=mesh, in_specs=in_specs, out_specs=out_specs, check_vma=False)
```

```python
import jax
import jax.numpy as jnp
from jax import lax
from jax.experimental import pallas as pl
from jax.experimental.pallas import tpu as pltpu
from jax.sharding import PartitionSpec as P

ROUTE_SCALE = 2.5
EPSILON = 1e-06
PAD = 128
RING = 4


def attn_pairs(stage, step):
    pairs = []
    for y in range(RING):
        for z in range(RING):
            for core in range(2):
                to = [y, z, core]
                if stage == "core":
                    to[2] = 1 - core
                else:
                    axis = stage if core == 0 else 1 - stage
                    to[axis] = (to[axis] + step) % RING
                pairs.append(((y * RING + z) * 2 + core, (to[0] * RING + to[1]) * 2 + to[2]))
    return pairs


def move(value, axis, step):
    if axis == "x":
        return lax.ppermute(value, "exp", [(i, (i + step) % RING) for i in range(RING)])
    return lax.ppermute(value, "attn", attn_pairs(axis, step))


def direct(chunks, axis):
    return [chunks[0], move(chunks[3], axis, -1), move(chunks[2], axis, 2), move(chunks[1], axis, 1)]


def gather_ring(value, axis):
    half = value.shape[0] // 2
    low = move(value, axis, 1)
    high = move(value, axis, -1)
    first = move(low[:half], axis, 1)
    second = move(high[half:], axis, -1)
    return [value, high, first, second, low]


def add(one, other):
    return (one.astype(jnp.float32) + other.astype(jnp.float32)).astype(jnp.bfloat16)


def scatter_ring(own, chunks, axis):
    half = chunks[1].shape[0] // 2
    first = move(chunks[1][:half], axis, 1)
    second = move(chunks[1][half:], axis, -1)
    up = jnp.concatenate([add(chunks[0][:half], first), chunks[0][half:]], axis=0)
    down = jnp.concatenate([chunks[2][:half], add(chunks[2][half:], second)], axis=0)
    low = move(up, axis, 1)
    high = move(down, axis, -1)
    total = own.astype(jnp.float32) + low.astype(jnp.float32) + high.astype(jnp.float32)
    return total.astype(jnp.bfloat16)


def prepare_kernel(place_ref, hidden_ref, gain_ref, routes_ref, scores_ref, capacity_ref, *out_refs):
    rows, top = routes_ref.shape
    experts = capacity_ref.shape[1]
    width = out_refs[0].shape[1] - PAD
    hidden = hidden_ref[...].astype(jnp.float32)
    scale = lax.rsqrt(jnp.mean(hidden * hidden, axis=1, keepdims=True) + EPSILON)
    routes = routes_ref[...]
    scores = scores_ref[...]
    weights = ROUTE_SCALE * scores / jnp.sum(scores, axis=1, keepdims=True)
    lane = lax.broadcasted_iota(jnp.int32, (rows, PAD), 1)
    named = lax.rem(lane, experts)
    match = jnp.zeros((rows, PAD), jnp.float32)
    weight = jnp.zeros((rows, PAD), jnp.float32)
    for k in range(top):
        same = routes[:, k : k + 1] == named
        match = jnp.where(same, 1.0, match)
        weight = jnp.where(same, weights[:, k : k + 1], weight)
    row = lax.broadcasted_iota(jnp.int32, (rows, PAD), 0)
    rank = jnp.zeros((rows, PAD), jnp.float32)
    for j in range(rows):
        later = (row > j) & (row < (j // 4 + 1) * 4)
        rank = rank + jnp.where(later, match[j : j + 1, :], 0.0)
    spread = (
        lax.broadcasted_iota(jnp.int32, (experts, PAD), 0)
        == lax.rem(lax.broadcasted_iota(jnp.int32, (experts, PAD), 1), experts)
    ).astype(jnp.float32)
    limit = jnp.broadcast_to(capacity_ref[...].astype(jnp.float32), (8, experts))
    limit = jnp.dot(limit, spread, preferred_element_type=jnp.float32)[0:1]
    kept = (match > 0.0) & (rank < limit)
    high = weight.astype(jnp.bfloat16).astype(jnp.float32)
    group = lane // experts
    value = jnp.where(group == 0, rank + 1.0, jnp.where(group == 1, high, weight - high))
    columns = jnp.where(kept & (group < 3), value, 0.0).astype(jnp.bfloat16)
    for r in range(RING):
        start = pl.multiple_of(lax.rem(place_ref[0] + r, RING) * width, PAD)
        part = hidden_ref[:, pl.ds(start, width)].astype(jnp.float32) * scale * gain_ref[:, pl.ds(start, width)]
        out_refs[r][:, :width] = part.astype(jnp.bfloat16)
        out_refs[r][:, width:] = columns


def finish_kernel(place_ref, hidden_ref, *refs):
    out_ref = refs[-1]
    width = refs[0].shape[1]
    for r in range(RING):
        start = pl.multiple_of(lax.rem(place_ref[0] + r, RING) * width, PAD)
        total = hidden_ref[:, pl.ds(start, width)].astype(jnp.float32) + refs[r][...].astype(jnp.float32)
        out_ref[:, pl.ds(start, width)] = total.astype(jnp.bfloat16)


def specs(count):
    return [pl.BlockSpec(memory_space=pltpu.SMEM)] + [pl.BlockSpec(memory_space=pltpu.VMEM)] * count


def choose(picks, expert):
    lanes = jnp.arange(PAD)[None, :]
    code = jnp.sum(jnp.where(lanes == expert, picks, 0.0), axis=1)
    rows = picks.shape[0]
    per = rows // 16
    row = jnp.arange(rows, dtype=jnp.int32)
    slot = jnp.arange(rows // 2, dtype=jnp.int32)
    block = row % 32 // 8 * per + row // 32 * 2 + row % 8 // 4
    chosen = (block[:, None] == slot[None, :] // 2) & (
        code.astype(jnp.int32)[:, None] == (slot % 2 + 1)[None, :]
    )
    return chosen.astype(jnp.bfloat16)


def pick(chosen, rows):
    return lax.dot_general(
        chosen, rows, (((0,), (0,)), ((), ())), preferred_element_type=jnp.float32
    ).astype(jnp.bfloat16)


def hold(first, then):
    return lax.optimization_barrier((*first, *then))[len(first) :]


def shards(hidden, norm_gain, routes, route_scores, capacity, w_gate, w_up, w_down):
    experts = capacity.shape[0]
    expert = lax.axis_index("attn")
    other = expert + 1 - 2 * (expert % 2)
    place = lax.axis_index("exp").astype(jnp.int32).reshape(1)
    width = w_gate.shape[1]
    rows = hidden.shape[0]
    blocks = pl.pallas_call(
        prepare_kernel,
        out_shape=[jax.ShapeDtypeStruct((rows, width + PAD), jnp.bfloat16)] * RING,
        in_specs=specs(5),
        out_specs=[pl.BlockSpec(memory_space=pltpu.VMEM)] * RING,
        name="prepare",
    )(place, hidden, norm_gain.reshape(1, -1), routes, route_scores, capacity.reshape(1, -1))
    lane = jnp.arange(PAD)[None, :]
    mine = (lane == expert + experts) | (lane == expert + 2 * experts)

    def picks_of(lines):
        columns = lines[:, width:].astype(jnp.float32)
        theirs = move(pick(choose(columns, other), lines), "core", 1)
        return pick(choose(columns, expert), lines), theirs

    def enter(own, theirs, cuts):
        quarter = own.shape[0] // RING
        both = [value.reshape(RING, quarter, width + PAD) for value in (own, theirs)]
        slots = [value[:, low:high] for low, high in zip(cuts, cuts[1:] + [quarter]) for value in both]
        slots = jnp.concatenate(slots, axis=1).reshape(RING * 2 * quarter, width + PAD)
        scale = jnp.sum(jnp.where(mine, slots[:, width:].astype(jnp.float32), 0.0), axis=1)
        return slots[:, :width], scale

    def product(slots, weights):
        part = slots.shape[0] // RING
        value = jnp.dot(slots, weights[0], preferred_element_type=jnp.float32).astype(jnp.bfloat16)
        return [value[r * part : (r + 1) * part] for r in range(RING)]

    def sends(gate, gate_far, up, up_far):
        return (
            jnp.concatenate([add(gate[1], gate_far), up[1]], axis=0),
            jnp.concatenate([add(up[3], up_far), gate[3]], axis=0),
        )

    def activate(gate, up, low, high):
        part = gate.shape[0]
        low, high = low.astype(jnp.float32), high.astype(jnp.float32)
        gate_sum = gate.astype(jnp.float32) + low[:part] + high[part:]
        up_sum = up.astype(jnp.float32) + low[part:] + high[:part]
        return (jax.nn.silu(gate_sum) * up_sum).astype(jnp.bfloat16)

    def last(whole, scale):
        out = jnp.dot(whole, w_down[0], preferred_element_type=jnp.float32)
        return (out * scale[:, None]).astype(jnp.bfloat16).reshape(RING, -1, width)

    def leave(out, lines):
        columns = lines[:, width:].astype(jnp.float32)
        chosen = jnp.concatenate([choose(columns, expert), choose(columns, other)], axis=1)
        out = out.reshape(RING, 2, -1, width)
        theirs = move(out[:, 1].reshape(-1, width), "core", 1)
        returned = jnp.concatenate([out[:, 0].reshape(-1, width), theirs], axis=0)
        return jnp.dot(chosen, returned, preferred_element_type=jnp.float32).astype(jnp.bfloat16)

    lines = jnp.concatenate(direct(blocks, "x"), axis=0)
    near = jnp.concatenate(direct([lines] * RING, 0), axis=0)
    low, high = move(near, 1, 1), move(near, 1, -1)
    slots, near_scale = enter(*picks_of(near), [0])
    gate, up = product(slots, w_gate), product(slots, w_up)
    low, high, *near_parts = hold((), (low, high, *gate, *up))
    gate, up = near_parts[:RING], near_parts[RING:]
    half = near.shape[0] // 2
    first, second = move(low[:half], 1, 1), move(high[half:], 1, -1)
    gate_far, up_far = move(gate[2], "x", 1), move(up[2], "x", -1)
    two = jnp.concatenate([first, second], axis=0)
    one = jnp.concatenate([high, low], axis=0)
    far = jnp.concatenate([first, second, high, low], axis=0)
    own, theirs = picks_of(far)
    gate_far, up_far = hold((own,), (gate_far, up_far))
    to_low, to_high = sends(gate, gate_far, up, up_far)
    near_act = activate(gate[0], up[0], move(to_low, "x", 1), move(to_high, "x", -1))
    cut = near.shape[0] // 2 // RING
    slots, far_scale = enter(own, theirs, [0, cut])
    gate, up = product(slots, w_gate), product(slots, w_up)
    gate_far, up_far = move(gate[2], "x", 1), move(up[2], "x", -1)
    (near_act,) = hold(up, (near_act,))
    near_low, near_high = move(near_act, "x", 1), move(near_act, "x", -1)
    to_low, to_high = sends(gate, gate_far, up, up_far)
    to_low, to_high, near_low, near_high = hold((), (to_low, to_high, near_low, near_high))
    far_low, far_high = move(to_low, "x", 1), move(to_high, "x", -1)
    half = near_act.shape[0] // 2
    near_first, near_second = move(near_low[:half], "x", 1), move(near_high[half:], "x", -1)
    near_first, near_second = hold((far_low, far_high), (near_first, near_second))
    near_whole = jnp.concatenate([near_act, near_high, near_first, near_second, near_low], axis=0)
    pieces = gather_ring(activate(gate[0], up[0], far_low, far_high), "x")
    near_sum = leave(last(near_whole, near_scale), near)
    pieces = hold((near_sum,), pieces)
    out = last(jnp.concatenate(pieces, axis=0), far_scale)
    two_sum = leave(out[:, : 2 * cut], two)
    one_sum = leave(out[:, 2 * cut :], one)
    part = near.shape[0]
    summed = scatter_ring(near_sum, [one_sum[:part], two_sum, one_sum[part:]], 1)
    part = part // RING
    pieces = direct([summed[r * part : (r + 1) * part] for r in range(RING)], 0)
    summed = sum(piece.astype(jnp.float32) for piece in pieces).astype(jnp.bfloat16)
    back = direct([summed[r * rows : (r + 1) * rows] for r in range(RING)], "x")
    return pl.pallas_call(
        finish_kernel,
        out_shape=jax.ShapeDtypeStruct(hidden.shape, jnp.bfloat16),
        in_specs=specs(1 + RING),
        out_specs=pl.BlockSpec(memory_space=pltpu.VMEM),
        name="finish",
    )(place, hidden, *back)


def solution(mesh):
    in_specs = (
        P(("attn", "exp"), None),
        P(),
        P(("attn", "exp"), None),
        P(("attn", "exp"), None),
        P(),
        P("attn", "exp", None),
        P("attn", "exp", None),
        P("attn", None, "exp"),
    )
    out_specs = P(("attn", "exp"), None)
    return jax.shard_map(shards, mesh=mesh, in_specs=in_specs, out_specs=out_specs, check_vma=False)
```

```python
import jax
import jax.numpy as jnp
from jax import lax
from jax.experimental import pallas as pl
from jax.experimental.pallas import tpu as pltpu
from jax.sharding import PartitionSpec as P

ROUTE_SCALE = 2.5
EPSILON = 1e-06
PAD = 128
RING = 4


def attn_pairs(stage, step):
    pairs = []
    for y in range(RING):
        for z in range(RING):
            for core in range(2):
                to = [y, z, core]
                if stage == "core":
                    to[2] = 1 - core
                else:
                    axis = stage if core == 0 else 1 - stage
                    to[axis] = (to[axis] + step) % RING
                pairs.append(((y * RING + z) * 2 + core, (to[0] * RING + to[1]) * 2 + to[2]))
    return pairs


def move(value, axis, step):
    if axis == "x":
        return lax.ppermute(value, "exp", [(i, (i + step) % RING) for i in range(RING)])
    return lax.ppermute(value, "attn", attn_pairs(axis, step))


def swap(value):
    groups = []
    for core in range(2):
        for line in range(RING):
            near = [(a * RING + line if core == 0 else line * RING + a) * 2 + core for a in range(RING)]
            groups.append([attn * RING + x for attn in near for x in range(RING)])
    return lax.all_to_all(
        value, ("attn", "exp"), split_axis=0, concat_axis=0, axis_index_groups=groups, tiled=True
    )


def gather_ring(value, axis):
    half = value.shape[0] // 2
    low = move(value, axis, 1)
    high = move(value, axis, -1)
    first = move(low[:half], axis, 1)
    second = move(high[half:], axis, -1)
    return [value, high, first, second, low]


def add(one, other):
    return (one.astype(jnp.float32) + other.astype(jnp.float32)).astype(jnp.bfloat16)


def scatter_ring(own, chunks, axis):
    half = chunks[1].shape[0] // 2
    first = move(chunks[1][:half], axis, 1)
    second = move(chunks[1][half:], axis, -1)
    up = jnp.concatenate([add(chunks[0][:half], first), chunks[0][half:]], axis=0)
    down = jnp.concatenate([chunks[2][:half], add(chunks[2][half:], second)], axis=0)
    low = move(up, axis, 1)
    high = move(down, axis, -1)
    total = own.astype(jnp.float32) + low.astype(jnp.float32) + high.astype(jnp.float32)
    return total.astype(jnp.bfloat16)


def prepare_kernel(hidden_ref, gain_ref, routes_ref, scores_ref, capacity_ref, out_ref):
    rows, top = routes_ref.shape
    experts = capacity_ref.shape[1]
    hidden = hidden_ref[...].astype(jnp.float32)
    scale = lax.rsqrt(jnp.mean(hidden * hidden, axis=1, keepdims=True) + EPSILON)
    routes = routes_ref[...]
    scores = scores_ref[...]
    weights = ROUTE_SCALE * scores / jnp.sum(scores, axis=1, keepdims=True)
    lane = lax.broadcasted_iota(jnp.int32, (rows, PAD), 1)
    named = lax.rem(lane, experts)
    match = jnp.zeros((rows, PAD), jnp.float32)
    weight = jnp.zeros((rows, PAD), jnp.float32)
    for k in range(top):
        same = routes[:, k : k + 1] == named
        match = jnp.where(same, 1.0, match)
        weight = jnp.where(same, weights[:, k : k + 1], weight)
    row = lax.broadcasted_iota(jnp.int32, (rows, PAD), 0)
    rank = jnp.zeros((rows, PAD), jnp.float32)
    for j in range(rows):
        later = (row > j) & (row < (j // 4 + 1) * 4)
        rank = rank + jnp.where(later, match[j : j + 1, :], 0.0)
    spread = (
        lax.broadcasted_iota(jnp.int32, (experts, PAD), 0)
        == lax.rem(lax.broadcasted_iota(jnp.int32, (experts, PAD), 1), experts)
    ).astype(jnp.float32)
    limit = jnp.broadcast_to(capacity_ref[...].astype(jnp.float32), (8, experts))
    limit = jnp.dot(limit, spread, preferred_element_type=jnp.float32)[0:1]
    kept = (match > 0.0) & (rank < limit)
    high = weight.astype(jnp.bfloat16).astype(jnp.float32)
    group = lane // experts
    value = jnp.where(group == 0, rank + 1.0, jnp.where(group == 1, high, weight - high))
    columns = jnp.where(kept & (group < 3), value, 0.0).astype(jnp.bfloat16)
    width = out_ref.shape[2] - PAD
    for r in range(RING):
        cut = slice(r * width, (r + 1) * width)
        part = (hidden_ref[:, cut].astype(jnp.float32) * scale * gain_ref[:, cut]).astype(jnp.bfloat16)
        for a in range(RING):
            out_ref[a * RING + r, :, :width] = part
            out_ref[a * RING + r, :, width:] = columns


def finish_kernel(hidden_ref, back_ref, out_ref):
    width = back_ref.shape[2]
    for r in range(RING):
        cut = slice(r * width, (r + 1) * width)
        total = hidden_ref[:, cut].astype(jnp.float32)
        total += sum(back_ref[a * RING + r].astype(jnp.float32) for a in range(RING))
        out_ref[:, cut] = total.astype(jnp.bfloat16)


def choose(picks, expert, place):
    lanes = jnp.arange(PAD)[None, :]
    code = jnp.sum(jnp.where(lanes == expert, picks, 0.0), axis=1)
    rows = picks.shape[0]
    per = rows // 16
    row = jnp.arange(rows, dtype=jnp.int32)
    slot = jnp.arange(rows // 2, dtype=jnp.int32)
    turned = (row % 32 // 8 + RING - place) % RING
    block = turned * per + row // 32 * 2 + row % 8 // 4
    chosen = (block[:, None] == slot[None, :] // 2) & (
        code.astype(jnp.int32)[:, None] == (slot % 2 + 1)[None, :]
    )
    return chosen.astype(jnp.bfloat16)


def pick(chosen, rows):
    return lax.dot_general(
        chosen, rows, (((0,), (0,)), ((), ())), preferred_element_type=jnp.float32
    ).astype(jnp.bfloat16)


def hold(first, then):
    return lax.optimization_barrier((*first, *then))[len(first) :]


def shards(hidden, norm_gain, routes, route_scores, capacity, w_gate, w_up, w_down):
    experts = capacity.shape[0]
    expert = lax.axis_index("attn")
    other = expert + 1 - 2 * (expert % 2)
    place = lax.axis_index("exp")
    width = w_gate.shape[1]
    rows = hidden.shape[0]
    vmem = pl.BlockSpec(memory_space=pltpu.VMEM)
    blocks = pl.pallas_call(
        prepare_kernel,
        out_shape=jax.ShapeDtypeStruct((RING * RING, rows, width + PAD), jnp.bfloat16),
        in_specs=[vmem] * 5,
        out_specs=vmem,
        name="prepare",
    )(hidden, norm_gain.reshape(1, -1), routes, route_scores, capacity.reshape(1, -1))
    lane = jnp.arange(PAD)[None, :]
    mine = (lane == expert + experts) | (lane == expert + 2 * experts)

    def picks_of(lines):
        columns = lines[:, width:].astype(jnp.float32)
        theirs = move(pick(choose(columns, other, place), lines), "core", 1)
        return pick(choose(columns, expert, place), lines), theirs

    def enter(own, theirs, cuts):
        quarter = own.shape[0] // RING
        both = [value.reshape(RING, quarter, width + PAD) for value in (own, theirs)]
        slots = [value[:, low:high] for low, high in zip(cuts, cuts[1:] + [quarter]) for value in both]
        slots = jnp.concatenate(slots, axis=1).reshape(RING * 2 * quarter, width + PAD)
        scale = jnp.sum(jnp.where(mine, slots[:, width:].astype(jnp.float32), 0.0), axis=1)
        return slots[:, :width], scale

    def product(slots, weights):
        part = slots.shape[0] // RING
        value = jnp.dot(slots, weights[0], preferred_element_type=jnp.float32).astype(jnp.bfloat16)
        return [value[r * part : (r + 1) * part] for r in range(RING)]

    def sends(gate, gate_far, up, up_far):
        return (
            jnp.concatenate([add(gate[1], gate_far), up[1]], axis=0),
            jnp.concatenate([add(up[3], up_far), gate[3]], axis=0),
        )

    def activate(gate, up, low, high):
        part = gate.shape[0]
        low, high = low.astype(jnp.float32), high.astype(jnp.float32)
        gate_sum = gate.astype(jnp.float32) + low[:part] + high[part:]
        up_sum = up.astype(jnp.float32) + low[part:] + high[:part]
        return (jax.nn.silu(gate_sum) * up_sum).astype(jnp.bfloat16)

    def last(whole, scale):
        out = jnp.dot(whole, w_down[0], preferred_element_type=jnp.float32)
        return (out * scale[:, None]).astype(jnp.bfloat16).reshape(RING, -1, width)

    def leave(out, lines):
        columns = lines[:, width:].astype(jnp.float32)
        chosen = jnp.concatenate([choose(columns, expert, place), choose(columns, other, place)], axis=1)
        out = out.reshape(RING, 2, -1, width)
        theirs = move(out[:, 1].reshape(-1, width), "core", 1)
        returned = jnp.concatenate([out[:, 0].reshape(-1, width), theirs], axis=0)
        return jnp.dot(chosen, returned, preferred_element_type=jnp.float32).astype(jnp.bfloat16)

    near = swap(blocks).reshape(RING * RING * rows, width + PAD)
    low, high = move(near, 1, 1), move(near, 1, -1)
    slots, near_scale = enter(*picks_of(near), [0])
    gate, up = product(slots, w_gate), product(slots, w_up)
    low, high, *near_parts = hold((), (low, high, *gate, *up))
    gate, up = near_parts[:RING], near_parts[RING:]
    half = near.shape[0] // 2
    first, second = move(low[:half], 1, 1), move(high[half:], 1, -1)
    gate_far, up_far = move(gate[2], "x", 1), move(up[2], "x", -1)
    two = jnp.concatenate([first, second], axis=0)
    one = jnp.concatenate([high, low], axis=0)
    far = jnp.concatenate([first, second, high, low], axis=0)
    own, theirs = picks_of(far)
    gate_far, up_far = hold((own,), (gate_far, up_far))
    to_low, to_high = sends(gate, gate_far, up, up_far)
    near_act = activate(gate[0], up[0], move(to_low, "x", 1), move(to_high, "x", -1))
    cut = near.shape[0] // 2 // RING
    slots, far_scale = enter(own, theirs, [0, cut])
    gate, up = product(slots, w_gate), product(slots, w_up)
    gate_far, up_far = move(gate[2], "x", 1), move(up[2], "x", -1)
    (near_act,) = hold(up, (near_act,))
    near_low, near_high = move(near_act, "x", 1), move(near_act, "x", -1)
    to_low, to_high = sends(gate, gate_far, up, up_far)
    to_low, to_high, near_low, near_high = hold((), (to_low, to_high, near_low, near_high))
    far_low, far_high = move(to_low, "x", 1), move(to_high, "x", -1)
    half = near_act.shape[0] // 2
    near_first, near_second = move(near_low[:half], "x", 1), move(near_high[half:], "x", -1)
    near_first, near_second = hold((far_low, far_high), (near_first, near_second))
    near_whole = jnp.concatenate([near_act, near_high, near_first, near_second, near_low], axis=0)
    pieces = gather_ring(activate(gate[0], up[0], far_low, far_high), "x")
    near_sum = leave(last(near_whole, near_scale), near)
    pieces = hold((near_sum,), pieces)
    out = last(jnp.concatenate(pieces, axis=0), far_scale)
    two_sum = leave(out[:, : 2 * cut], two)
    one_sum = leave(out[:, 2 * cut :], one)
    part = near.shape[0]
    summed = scatter_ring(near_sum, [one_sum[:part], two_sum, one_sum[part:]], 1)
    back = swap(summed.reshape(RING * RING, rows, width))
    return pl.pallas_call(
        finish_kernel,
        out_shape=jax.ShapeDtypeStruct(hidden.shape, jnp.bfloat16),
        in_specs=[vmem] * 2,
        out_specs=vmem,
        name="finish",
    )(hidden, back)


def solution(mesh):
    in_specs = (
        P(("attn", "exp"), None),
        P(),
        P(("attn", "exp"), None),
        P(("attn", "exp"), None),
        P(),
        P("attn", "exp", None),
        P("attn", "exp", None),
        P("attn", None, "exp"),
    )
    out_specs = P(("attn", "exp"), None)
    return jax.shard_map(shards, mesh=mesh, in_specs=in_specs, out_specs=out_specs, check_vma=False)
```

```python
import jax
import jax.numpy as jnp
from jax import lax
from jax.experimental import pallas as pl
from jax.experimental.pallas import tpu as pltpu
from jax.sharding import PartitionSpec as P

ROUTE_SCALE = 2.5
EPSILON = 1e-06
PAD = 128
RING = 4


def attn_pairs(stage, step):
    pairs = []
    for y in range(RING):
        for z in range(RING):
            for core in range(2):
                to = [y, z, core]
                if stage == "core":
                    to[2] = 1 - core
                else:
                    axis = stage if core == 0 else 1 - stage
                    to[axis] = (to[axis] + step) % RING
                pairs.append(((y * RING + z) * 2 + core, (to[0] * RING + to[1]) * 2 + to[2]))
    return pairs


def move(value, axis, step):
    if axis == "x":
        return lax.ppermute(value, "exp", [(i, (i + step) % RING) for i in range(RING)])
    return lax.ppermute(value, "attn", attn_pairs(axis, step))


def swap(value):
    groups = []
    for core in range(2):
        for line in range(RING):
            near = [(a * RING + line if core == 0 else line * RING + a) * 2 + core for a in range(RING)]
            groups.append([attn * RING + x for attn in near for x in range(RING)])
    return lax.all_to_all(
        value, ("attn", "exp"), split_axis=0, concat_axis=0, axis_index_groups=groups, tiled=True
    )


def gather_ring(value, axis):
    half = value.shape[0] // 2
    low = move(value, axis, 1)
    high = move(value, axis, -1)
    first = move(low[:half], axis, 1)
    second = move(high[half:], axis, -1)
    return [value, high, first, second, low]


def add(one, other):
    return (one.astype(jnp.float32) + other.astype(jnp.float32)).astype(jnp.bfloat16)


def scatter_ring(own, chunks, axis):
    half = chunks[1].shape[0] // 2
    first = move(chunks[1][:half], axis, 1)
    second = move(chunks[1][half:], axis, -1)
    up = jnp.concatenate([add(chunks[0][:half], first), chunks[0][half:]], axis=0)
    down = jnp.concatenate([chunks[2][:half], add(chunks[2][half:], second)], axis=0)
    low = move(up, axis, 1)
    high = move(down, axis, -1)
    total = own.astype(jnp.float32) + low.astype(jnp.float32) + high.astype(jnp.float32)
    return total.astype(jnp.bfloat16)


def prepare_kernel(hidden_ref, gain_ref, routes_ref, scores_ref, capacity_ref, out_ref):
    rows, top = routes_ref.shape
    experts = capacity_ref.shape[1]
    hidden = hidden_ref[...].astype(jnp.float32)
    scale = lax.rsqrt(jnp.mean(hidden * hidden, axis=1, keepdims=True) + EPSILON)
    routes = routes_ref[...]
    scores = scores_ref[...]
    weights = ROUTE_SCALE * scores / jnp.sum(scores, axis=1, keepdims=True)
    lane = lax.broadcasted_iota(jnp.int32, (rows, PAD), 1)
    named = lax.rem(lane, experts)
    match = jnp.zeros((rows, PAD), jnp.float32)
    weight = jnp.zeros((rows, PAD), jnp.float32)
    for k in range(top):
        same = routes[:, k : k + 1] == named
        match = jnp.where(same, 1.0, match)
        weight = jnp.where(same, weights[:, k : k + 1], weight)
    row = lax.broadcasted_iota(jnp.int32, (rows, PAD), 0)
    rank = jnp.zeros((rows, PAD), jnp.float32)
    for j in range(rows):
        later = (row > j) & (row < (j // 4 + 1) * 4)
        rank = rank + jnp.where(later, match[j : j + 1, :], 0.0)
    spread = (
        lax.broadcasted_iota(jnp.int32, (experts, PAD), 0)
        == lax.rem(lax.broadcasted_iota(jnp.int32, (experts, PAD), 1), experts)
    ).astype(jnp.float32)
    limit = jnp.broadcast_to(capacity_ref[...].astype(jnp.float32), (8, experts))
    limit = jnp.dot(limit, spread, preferred_element_type=jnp.float32)[0:1]
    kept = (match > 0.0) & (rank < limit)
    high = weight.astype(jnp.bfloat16).astype(jnp.float32)
    group = lane // experts
    value = jnp.where(group == 0, rank + 1.0, jnp.where(group == 1, high, weight - high))
    columns = jnp.where(kept & (group < 3), value, 0.0).astype(jnp.bfloat16)
    width = out_ref.shape[2] - PAD
    for r in range(RING):
        cut = slice(r * width, (r + 1) * width)
        part = (hidden_ref[:, cut].astype(jnp.float32) * scale * gain_ref[:, cut]).astype(jnp.bfloat16)
        for a in range(RING):
            out_ref[a * RING + r, :, :width] = part
            out_ref[a * RING + r, :, width:] = columns


def finish_kernel(hidden_ref, back_ref, out_ref):
    width = back_ref.shape[2]
    for r in range(RING):
        cut = slice(r * width, (r + 1) * width)
        total = hidden_ref[:, cut].astype(jnp.float32)
        total += sum(back_ref[a * RING + r].astype(jnp.float32) for a in range(RING))
        out_ref[:, cut] = total.astype(jnp.bfloat16)


def choose(picks, expert, place):
    lanes = jnp.arange(PAD)[None, :]
    code = jnp.sum(jnp.where(lanes == expert, picks, 0.0), axis=1)
    rows = picks.shape[0]
    per = rows // 16
    row = jnp.arange(rows, dtype=jnp.int32)
    slot = jnp.arange(rows // 2, dtype=jnp.int32)
    turned = (row % 32 // 8 + RING - place) % RING
    block = turned * per + row // 32 * 2 + row % 8 // 4
    chosen = (block[:, None] == slot[None, :] // 2) & (
        code.astype(jnp.int32)[:, None] == (slot % 2 + 1)[None, :]
    )
    return chosen.astype(jnp.bfloat16)


def pick(chosen, rows):
    return lax.dot_general(
        chosen, rows, (((0,), (0,)), ((), ())), preferred_element_type=jnp.float32
    ).astype(jnp.bfloat16)


def hold(first, then):
    return lax.optimization_barrier((*first, *then))[len(first) :]


def shards(hidden, norm_gain, routes, route_scores, capacity, w_gate, w_up, w_down):
    experts = capacity.shape[0]
    expert = lax.axis_index("attn")
    other = expert + 1 - 2 * (expert % 2)
    place = lax.axis_index("exp")
    width = w_gate.shape[1]
    rows = hidden.shape[0]
    vmem = pl.BlockSpec(memory_space=pltpu.VMEM)
    blocks = pl.pallas_call(
        prepare_kernel,
        out_shape=jax.ShapeDtypeStruct((RING * RING, rows, width + PAD), jnp.bfloat16),
        in_specs=[vmem] * 5,
        out_specs=vmem,
        name="prepare",
    )(hidden, norm_gain.reshape(1, -1), routes, route_scores, capacity.reshape(1, -1))
    lane = jnp.arange(PAD)[None, :]
    mine = (lane == expert + experts) | (lane == expert + 2 * experts)

    def picks_of(lines):
        columns = lines[:, width:].astype(jnp.float32)
        theirs = move(pick(choose(columns, other, place), lines), "core", 1)
        return pick(choose(columns, expert, place), lines), theirs

    def enter(own, theirs, cuts):
        quarter = own.shape[0] // RING
        both = [value.reshape(RING, quarter, width + PAD) for value in (own, theirs)]
        slots = [value[:, low:high] for low, high in zip(cuts, cuts[1:] + [quarter]) for value in both]
        slots = jnp.concatenate(slots, axis=1).reshape(RING * 2 * quarter, width + PAD)
        scale = jnp.sum(jnp.where(mine, slots[:, width:].astype(jnp.float32), 0.0), axis=1)
        return slots[:, :width], scale

    def product(slots, weights):
        part = slots.shape[0] // RING
        value = jnp.dot(slots, weights[0], preferred_element_type=jnp.float32).astype(jnp.bfloat16)
        return [value[r * part : (r + 1) * part] for r in range(RING)]

    def sends(gate, gate_far, up, up_far):
        return (
            jnp.concatenate([add(gate[1], gate_far), up[1]], axis=0),
            jnp.concatenate([add(up[3], up_far), gate[3]], axis=0),
        )

    def activate(gate, up, low, high):
        part = gate.shape[0]
        low, high = low.astype(jnp.float32), high.astype(jnp.float32)
        gate_sum = gate.astype(jnp.float32) + low[:part] + high[part:]
        up_sum = up.astype(jnp.float32) + low[part:] + high[:part]
        return (jax.nn.silu(gate_sum) * up_sum).astype(jnp.bfloat16)

    def last(whole, scale):
        out = jnp.dot(whole, w_down[0], preferred_element_type=jnp.float32)
        return (out * scale[:, None]).astype(jnp.bfloat16).reshape(RING, -1, width)

    def leave(out, lines):
        columns = lines[:, width:].astype(jnp.float32)
        chosen = jnp.concatenate([choose(columns, expert, place), choose(columns, other, place)], axis=1)
        out = out.reshape(RING, 2, -1, width)
        theirs = move(out[:, 1].reshape(-1, width), "core", 1)
        returned = jnp.concatenate([out[:, 0].reshape(-1, width), theirs], axis=0)
        return jnp.dot(chosen, returned, preferred_element_type=jnp.float32).astype(jnp.bfloat16)

    near = swap(blocks).reshape(RING * RING * rows, width + PAD)
    low, high = move(near, 1, 1), move(near, 1, -1)
    slots, near_scale = enter(*picks_of(near), [0])
    gate, up = product(slots, w_gate), product(slots, w_up)
    low, high, *near_parts = hold((), (low, high, *gate, *up))
    gate, up = near_parts[:RING], near_parts[RING:]
    half = near.shape[0] // 2
    first, second = move(low[:half], 1, 1), move(high[half:], 1, -1)
    gate_far, up_far = move(gate[2], "x", 1), move(up[2], "x", -1)
    two = jnp.concatenate([first, second], axis=0)
    one = jnp.concatenate([high, low], axis=0)
    far = jnp.concatenate([first, second, high, low], axis=0)
    own, theirs = picks_of(far)
    near_gate, near_up, near_fars = gate, up, (gate_far, up_far)
    cut = near.shape[0] // 2 // RING
    slots, far_scale = enter(own, theirs, [0, cut])
    gate, up = product(slots, w_gate), product(slots, w_up)
    gate_far, up_far = move(gate[2], "x", 1), move(up[2], "x", -1)
    far_sends = sends(gate, gate_far, up, up_far)
    far_low, far_high = move(far_sends[0], "x", 1), move(far_sends[1], "x", -1)
    near_fars = hold(far_sends, near_fars)
    near_sends = sends(near_gate, near_fars[0], near_up, near_fars[1])
    near_low, near_high = move(near_sends[0], "x", 1), move(near_sends[1], "x", -1)
    far_act = activate(gate[0], up[0], far_low, far_high)
    far_low, far_high = move(far_act, "x", 1), move(far_act, "x", -1)
    near_low, near_high = hold((far_act,), (near_low, near_high))
    near_act = activate(near_gate[0], near_up[0], near_low, near_high)
    near_low, near_high = move(near_act, "x", 1), move(near_act, "x", -1)
    half = far_act.shape[0] // 2
    far_first, far_second = move(far_low[:half], "x", 1), move(far_high[half:], "x", -1)
    near_low, near_high = hold((far_low, far_high), (near_low, near_high))
    half = near_act.shape[0] // 2
    near_first, near_second = move(near_low[:half], "x", 1), move(near_high[half:], "x", -1)
    out = last(jnp.concatenate([far_act, far_high, far_first, far_second, far_low], axis=0), far_scale)
    near_first, near_second = hold((out,), (near_first, near_second))
    near_whole = jnp.concatenate([near_act, near_high, near_first, near_second, near_low], axis=0)
    near_sum = leave(last(near_whole, near_scale), near)
    two_sum = leave(out[:, : 2 * cut], two)
    one_sum = leave(out[:, 2 * cut :], one)
    part = near.shape[0]
    summed = scatter_ring(near_sum, [one_sum[:part], two_sum, one_sum[part:]], 1)
    back = swap(summed.reshape(RING * RING, rows, width))
    return pl.pallas_call(
        finish_kernel,
        out_shape=jax.ShapeDtypeStruct(hidden.shape, jnp.bfloat16),
        in_specs=[vmem] * 2,
        out_specs=vmem,
        name="finish",
    )(hidden, back)


def solution(mesh):
    in_specs = (
        P(("attn", "exp"), None),
        P(),
        P(("attn", "exp"), None),
        P(("attn", "exp"), None),
        P(),
        P("attn", "exp", None),
        P("attn", "exp", None),
        P("attn", None, "exp"),
    )
    out_specs = P(("attn", "exp"), None)
    return jax.shard_map(shards, mesh=mesh, in_specs=in_specs, out_specs=out_specs, check_vma=False)
```
